32 devices in a mesh: aa: 8 (over y, x, core), ba: 4 (over z).
Axes of the slice: x: 2, y: 2, z: 4, core: 2. Of those that a mesh axis runs over, the one named last changes fastest.
Arguments:
- amplitudes: bfloat16 [512, 512], P('aa', 'ba'), may hold values from -6 to 6
- code: int32 [32, 512], replicated, may hold values from -512 to 512, as said below
- counts: int32 [32], replicated, may hold values from 1 to 16, as said below
- pair_irrep: int32 [32], replicated, may hold values from 0 to 7
- integrals: bfloat16 [32, 32], replicated, may hold values from -3 to 3
- one_body: bfloat16 [32], replicated, may hold values from -1.5 to 1.5
Outputs:
- sigma: bfloat16 [512, 512], P('aa', 'ba')
The draws below stay inside these ranges and needn't reach their ends.
Inputs may be any that keep to these rules, and one draw needn't show every extreme that they name: |code| - 1 names the target string of a replacement and the sign of code its sign; some entries reach both ends. `counts`: the live strings of fine block j fill its first slots, from slot j * 16 on; in every draw some block is full and some holds one string.
All inputs are finite; a program needn't handle non-finite values.
Results may differ from the reference program's by a relative error of at most 0.0045.
Values may be sent and summed in bfloat16 or wider, within the bound.
No kernel may reach another device: no remote copies, remote signals or barrier semaphores. Data moves between devices by JAX's collectives and lax.ppermute only.
A program may use at most 128 MiB of HBM per device.

```python
import jax
import jax.numpy as jnp
from jax import lax

CAP = 16
PAIRS = 32
IRREPS = 8
BLOCKS = 32
NS = 512


def draw_code(key, part):
    keys = jax.random.split(jax.random.fold_in(key, 11), 3)
    keep = jax.random.randint(keys[0], (PAIRS, NS), 0, 2)
    target = jax.random.randint(keys[1], (PAIRS, NS), 0, NS)
    sign = 2 * jax.random.randint(keys[2], (PAIRS, NS), 0, 2) - 1
    code = keep * sign * (target + 1)
    code = code.at[0, 0].set(NS).at[0, 1].set(0 - NS)
    return code.astype(jnp.int32)


def draw_counts(key, part):
    keys = jax.random.split(jax.random.fold_in(key, 23), 3)
    values = jax.random.randint(keys[0], (BLOCKS,), 1, CAP + 1)
    first = jax.random.randint(keys[1], (), 0, BLOCKS)
    step = jax.random.randint(keys[2], (), 1, BLOCKS)
    second = (first + step) % BLOCKS
    values = values.at[first].set(CAP).at[second].set(1)
    return values.astype(jnp.int32)


def place_ends(array, key, least, top_value):
    dims = array.shape
    place = [jax.random.randint(jax.random.fold_in(key, axis), (), 0, dims[axis]) for axis in range(len(dims))]
    array = array.at[tuple(place)].set(least)
    longest = dims.index(max(dims))
    place[longest] = (place[longest] + 1) % dims[longest]
    return array.at[tuple(place)].set(top_value)


def steps_of(own_key, extent, cuts, smallest, high):
    gain = 1.0
    for dim, parts in cuts:
        steps = jax.random.uniform(jax.random.fold_in(jax.random.fold_in(own_key, 6), dim), (parts,), jnp.float32, smallest / len(cuts), high / len(cuts))
        gain = gain * jnp.repeat(jnp.exp(steps), extent[dim] // parts).reshape((-1,) + (1,) * (len(extent) - 1 - dim))
    return gain


def bell_draw(rng, shape, spread, bound, shards=(), held_as=jnp.bfloat16):
    values = jax.random.normal(rng, shape, jnp.float32) * spread
    if len(shards) > 0:
        values = steps_of(rng, shape, shards, -0.22, 0.18) * values
    return jnp.clip(values, min=-bound, max=bound).astype(held_as)


def setup_inputs(seed: int = 0) -> dict:
    key_of = jax.random.split(jax.random.key(seed), 7)
    return {
        "amplitudes": bell_draw(key_of[0], (NS, NS), 1.0, 6.0, ((0, 8), (1, 4))),
        "code": draw_code(jax.random.fold_in(key_of[6], 71), 0),
        "counts": draw_counts(jax.random.fold_in(key_of[6], 71), 0),
        "pair_irrep": place_ends(jax.random.randint(key_of[3], (PAIRS,), 0, IRREPS), jax.random.fold_in(key_of[3], 1), 0, IRREPS - 1).astype(jnp.int32),
        "integrals": bell_draw(key_of[4], (PAIRS, PAIRS), (PAIRS // 8) ** -0.5, 3.0),
        "one_body": bell_draw(key_of[5], (PAIRS,), 0.25, 1.5),
    }


def live_of(counts):
    slots = jnp.arange(NS, dtype=jnp.int32)
    return (slots % CAP < counts[slots // CAP]).astype(jnp.float32)


def reference(amplitudes, code, counts, pair_irrep, integrals, one_body):
    live = live_of(counts)
    masked = (amplitudes.astype(jnp.float32) * (live[:, None] * live[None, :])).astype(jnp.bfloat16)
    masked_wide = masked.astype(jnp.float32)
    target = jnp.maximum(jnp.abs(code) - 1, 0).astype(jnp.int32)
    signs = jnp.sign(code).astype(jnp.float32)
    weights = jnp.where(pair_irrep[:, None] == pair_irrep[None, :], integrals, jnp.zeros((), integrals.dtype))
    order = jnp.arange(PAIRS, dtype=jnp.int32)

    def beta_side(pair):
        return (masked_wide[:, target[pair]] * (signs[pair] * live)[None, :]).astype(jnp.bfloat16)

    def alpha_side(pair):
        return (masked_wide[target[pair], :] * (signs[pair] * live)[:, None]).astype(jnp.bfloat16)

    dbeta = lax.map(beta_side, order)
    dalpha = lax.map(alpha_side, order)
    flat_beta = dbeta.reshape(PAIRS, NS * NS)
    flat_alpha = dalpha.reshape(PAIRS, NS * NS)
    gains = one_body.astype(jnp.float32)

    def accumulate(total, pair):
        row = lax.dynamic_slice_in_dim(weights, pair, 1, 0)
        gbeta_full = jnp.dot(row, flat_beta, preferred_element_type=jnp.float32).reshape(NS, NS)
        galpha_full = jnp.dot(row, flat_alpha, preferred_element_type=jnp.float32).reshape(NS, NS)
        gbeta_wide = gbeta_full.astype(jnp.bfloat16).astype(jnp.float32)
        combined_wide = (gbeta_full + 0.5 * galpha_full).astype(jnp.bfloat16).astype(jnp.float32)
        tgt = target[pair]
        sgn = signs[pair]
        total = total + gains[pair] * (dbeta[pair].astype(jnp.float32) + dalpha[pair].astype(jnp.float32))
        total = total + sgn[None, :] * (0.5 * gbeta_wide[:, tgt])
        total = total + sgn[:, None] * combined_wide[tgt, :]
        return total, None

    total, _ = lax.scan(accumulate, jnp.zeros((NS, NS), jnp.float32), order)
    return (total * (live[:, None] * live[None, :])).astype(jnp.bfloat16)
```

```python
import functools

import jax
import jax.numpy as jnp
from jax import lax
from jax.experimental import pallas as pl
from jax.experimental.pallas import tpu as pltpu
from jax.sharding import PartitionSpec as P

BF16 = jnp.bfloat16
F32 = jnp.float32
I32 = jnp.int32
RESIDENT = 8 * 2**20
VMEM_LIMIT = 48 * 2**20


def iota(shape, dim):
    return lax.broadcasted_iota(I32, shape, dim)


def dot(x, y):
    return jnp.dot(x, y, preferred_element_type=F32)


def dot_nt(x, y):
    return lax.dot_general(x, y, (((1,), (1,)), ((), ())), preferred_element_type=F32)


def live_ids(counts_ref, first, shape, dim, cap):
    ids = iota(shape, dim)
    block = ids // cap
    count = jnp.zeros(shape, I32)
    for j in range(shape[dim] // cap):
        count = jnp.where(block == j, counts_ref[first // cap + j], count)
    return jnp.where(ids - block * cap < count, ids + first + 1, -1)


def sign_of(code):
    return jnp.where(code > 0, 1.0, -1.0).astype(F32)


def mix_kernel(steps, cap, start, counts_ref, irrep_ref, code_ref, integrals_ref, gains_ref, mixed_ref, one_ref):
    pairs, strings = code_ref.shape
    rows = one_ref.shape[0]
    step = 0 if steps == 1 else pl.program_id(0)
    wide = pairs * 8
    ids = live_ids(counts_ref, 0, (1, strings), 1, cap)
    irrep_p = jnp.zeros((pairs, pairs), I32)
    irrep_q = jnp.zeros((pairs, pairs), I32)
    for p in range(pairs):
        irrep_p = jnp.where(iota((pairs, pairs), 0) == p, irrep_ref[p], irrep_p)
        irrep_q = jnp.where(iota((pairs, pairs), 1) == p, irrep_ref[p], irrep_q)
    weights = jnp.where(irrep_p == irrep_q, integrals_ref[...].astype(F32), 0.0).astype(BF16)
    spread_q = jnp.where(iota((wide, pairs), 0) // 8 == iota((wide, pairs), 1), 1.0, 0.0).astype(BF16)
    spread_p = jnp.where(iota((pairs, wide), 1) % pairs == iota((pairs, wide), 0), 1.0, 0.0).astype(BF16)
    left = jnp.concatenate(
        [dot_nt(spread_q, weights), jnp.broadcast_to(gains_ref[...].astype(F32), (8, pairs))], 0
    ).astype(BF16)
    mixer = dot(left, spread_p)
    same = iota(mixer.shape, 0) % 8 == iota(mixer.shape, 1) // pairs
    mixer = jnp.where(same, mixer, 0.0).astype(BF16)
    first = pl.multiple_of(start(step), 128)
    code = code_ref[:, pl.ds(first, rows)]
    size = jnp.abs(code)
    sign = sign_of(code)
    for base in range(0, rows, 16):
        halves = []
        for low in (base, base + 8):
            hot = jnp.concatenate(
                [
                    jnp.where(size[:, a : a + 1] == ids, sign[:, a : a + 1], 0.0).astype(BF16)
                    for a in range(low, low + 8)
                ],
                0,
            )
            part = dot(mixer, hot)
            one_ref[pl.ds(low, 8), :] = part[wide:]
            halves.append(part[:wide].reshape(pairs, 8, strings))
        mixed_ref[:, pl.ds(base, 16), :] = jnp.concatenate(halves, 1).astype(BF16)


def same_spin_kernel(steps, cap, origin, counts_ref, code_ref, mixed_ref, one_ref, low_ref, high_ref, hot_ref, message_ref, total_ref):
    pairs, rows, strings = mixed_ref.shape
    columns = low_ref.shape[1]
    step = 0 if steps == 1 else pl.program_id(0)
    first_a, first_b = origin()
    ids = live_ids(counts_ref, first_b, (columns, 128), 0, cap)
    ids = jnp.concatenate([ids] * (strings // 128), 1)

    @pl.when(step == 0)
    def _():
        total_ref[...] = jnp.zeros_like(total_ref)

    total = total_ref[...]
    for q in range(pairs):
        code = code_ref[q : q + 1, :]
        hot = jnp.where(jnp.abs(code) == ids, sign_of(code), 0.0).astype(BF16)
        hot_ref[pl.ds(q * columns, columns), :] = hot
        total = total + dot_nt(mixed_ref[q], hot)
    total_ref[...] = total

    @pl.when(step == steps - 1)
    def _():
        half = low_ref.shape[0]
        message_ref[:half] = low_ref[...]
        message_ref[half : 2 * half] = high_ref[...]
        one = one_ref[:, pl.ds(pl.multiple_of(first_b, 128), columns)]
        message_ref[2 * half :] = (one + 0.5 * total_ref[...]).astype(BF16)


def mixed_kernel(steps, groups, peers, place, mixed_ref, hot_ref, *refs):
    arrived = refs[:groups]
    own_ref, amplitudes_ref = refs[groups : groups + 2]
    sent = refs[groups + 2 : groups + 1 + peers]
    all_f, line, total_ref = refs[groups + 1 + peers :]
    pairs, rows, strings = mixed_ref.shape[0], own_ref.shape[0], mixed_ref.shape[2]
    columns = own_ref.shape[1]
    chip = 2 * rows
    step = 0 if steps == 1 else pl.program_id(0)
    group, core, column = place()

    @pl.when(step == 0)
    def _():
        for k in range(groups):
            at = pl.multiple_of((group ^ k) * chip, chip)
            amplitudes_ref[pl.ds(at, chip), :] = arrived[k][:chip]
            all_f[pl.ds(at, chip), :] = arrived[k][chip:]
        at = pl.multiple_of(core * rows, rows)
        total_ref[...] = dot_nt(arrived[0][pl.ds(at, rows), :], all_f[...])

    amplitudes = amplitudes_ref[...]
    at = pl.multiple_of(core * rows, rows) if mixed_ref.shape[1] != rows else 0
    for q in range(pairs):
        part = dot(mixed_ref[q, pl.ds(at, rows), :], amplitudes)
        line[:, pl.ds(q * columns, columns)] = part.astype(BF16)
    total_ref[...] += dot(line[...], hot_ref[...])

    @pl.when(step == steps - 1)
    def _():
        own_f = arrived[0][pl.ds(pl.multiple_of(chip + core * rows, rows), rows), :]
        for k in range(peers):
            part = total_ref[:, pl.ds(pl.multiple_of((column ^ k) * columns, columns), columns)]
            if k == 0:
                own_ref[...] = part
            else:
                sent[k - 1][:rows] = part.astype(BF16)
                sent[k - 1][rows:] = own_f


def final_kernel(groups, peers, cap, place, counts_ref, own_ref, amplitudes_ref, message_ref, *refs):
    arrived, out_ref = refs[:-1], refs[-1]
    rows, columns = own_ref.shape
    chip = 2 * rows
    first_a, core, column = place()
    total = own_ref[...]
    own_f = message_ref[pl.ds(pl.multiple_of(chip + core * rows, rows), rows), :]
    for k in range(peers):
        block = amplitudes_ref[pl.ds(pl.multiple_of((column ^ k) * columns, columns), columns), :]
        if k == 0:
            total = total + dot(own_f, block)
        else:
            total = total + arrived[k - 1][:rows].astype(F32) + dot(arrived[k - 1][rows:], block)
    live_a = live_ids(counts_ref, first_a, (rows, columns), 0, cap)
    live_b = live_ids(counts_ref, column * columns, (1, columns), 1, cap)
    out_ref[...] = jnp.where((live_a > 0) & (live_b > 0), total, 0.0).astype(BF16)


def per_device(sizes, amplitudes, code, counts, pair_irrep, integrals, one_body):
    rows, columns = amplitudes.shape
    pairs, strings = code.shape
    cap = strings // counts.shape[0]
    groups, peers = sizes[0] // 2, sizes[1]
    chip = 2 * rows
    names = ("aa", "ba")
    resident = pairs * chip * strings * 2 <= RESIDENT
    row_tiles = 1 if resident else chip // 128
    pair_tiles = 1 if resident else pairs // 4
    smem = pl.BlockSpec(memory_space=pltpu.SMEM)

    def whole():
        return pl.BlockSpec(memory_space=pltpu.VMEM)

    def tiled(shape, dim):
        if resident:
            return whole()
        return pl.BlockSpec(shape, lambda i: tuple(i if d == dim else 0 for d in range(len(shape))))

    def shape_of(shape, dtype):
        return pltpu.VMEM(shape, dtype) if resident else jax.ShapeDtypeStruct(shape, dtype)

    def near(value):
        return pltpu.with_memory_space_constraint(value, pltpu.VMEM) if resident else value

    def call(body, name, tiles, *args, **keys):
        if tiles > 1:
            keys["grid"] = (tiles,)
        params = pltpu.CompilerParams(vmem_limit_bytes=VMEM_LIMIT)
        return pl.pallas_call(body, name=name, compiler_params=params, **keys)(*args)

    def group_at():
        return lax.axis_index("aa") // 2

    def send(value, axis, mask):
        size = lax.axis_size(axis)
        return lax.ppermute(value, axis, [(i, i ^ mask) for i in range(size)])

    def kernel(body, *static):
        return functools.partial(body, *static)

    sibling = send(amplitudes, "aa", 1)
    tile = chip // row_tiles
    mixed, one = call(
        kernel(mix_kernel, row_tiles, cap, lambda step: group_at() * chip + step * tile),
        "mix",
        row_tiles,
        counts,
        pair_irrep,
        code,
        integrals,
        one_body.reshape(1, pairs),
        in_specs=[smem, smem, whole(), whole(), whole()],
        out_shape=(shape_of((pairs, chip, strings), BF16), shape_of((chip, strings), F32)),
        out_specs=(tiled((pairs, tile, strings), 1), tiled((tile, strings), 0)),
    )
    first = lax.axis_index("aa") % 2 == 0
    low = jnp.where(first, amplitudes, sibling)
    high = jnp.where(first, sibling, amplitudes)
    part = pairs // pair_tiles
    hot, message = call(
        kernel(same_spin_kernel, pair_tiles, cap, lambda: (group_at() * chip, lax.axis_index("ba") * columns)),
        "same_spin",
        pair_tiles,
        counts,
        code if pair_tiles == 1 else code.reshape(pair_tiles, part, strings),
        near(mixed),
        near(one),
        low,
        high,
        in_specs=[
            smem,
            whole() if pair_tiles == 1 else pl.BlockSpec((None, part, strings), lambda i: (i, 0, 0)),
            tiled((part, chip, strings), 0),
            whole(),
            whole(),
            whole(),
        ],
        out_shape=(shape_of((pairs * columns, strings), BF16), shape_of((2 * chip, columns), BF16)),
        out_specs=(tiled((part * columns, strings), 0), whole()),
        scratch_shapes=[pltpu.VMEM((chip, columns), F32)],
    )
    messages = [message] + [send(message, "aa", 2 * k) for k in range(1, groups)]
    core_of = lambda: lax.axis_index("aa") % 2
    outs = call(
        kernel(mixed_kernel, pair_tiles, groups, peers, lambda: (group_at(), core_of(), lax.axis_index("ba"))),
        "mixed",
        pair_tiles,
        near(mixed),
        near(hot),
        *[near(m) for m in messages],
        in_specs=[tiled((part, chip, strings), 0), tiled((part * columns, strings), 0)] + [whole()] * groups,
        out_shape=(shape_of((rows, columns), F32), shape_of((strings, columns), BF16))
        + tuple(shape_of((2 * rows, columns), BF16) for _ in range(peers - 1)),
        out_specs=tuple(whole() for _ in range(peers + 1)),
        scratch_shapes=[
            pltpu.VMEM((strings, columns), BF16),
            pltpu.VMEM((rows, part * columns), BF16),
            pltpu.VMEM((rows, strings), F32),
        ],
    )
    own, gathered = outs[:2]
    arrived = [send(m, "ba", k + 1) for k, m in enumerate(outs[2:])]
    return call(
        kernel(final_kernel, groups, peers, cap, lambda: (lax.axis_index("aa") * rows, core_of(), lax.axis_index("ba"))),
        "final",
        1,
        counts,
        near(own),
        near(gathered),
        near(message),
        *[near(m) for m in arrived],
        in_specs=[smem] + [whole()] * (2 + peers),
        out_shape=jax.ShapeDtypeStruct((rows, columns), BF16),
        out_specs=whole(),
    )


def solution(mesh):
    placed = (P("aa", "ba"), P(), P(), P(), P(), P())
    sizes = (mesh.shape["aa"], mesh.shape["ba"])
    return jax.shard_map(
        functools.partial(per_device, sizes), mesh=mesh, in_specs=placed, out_specs=P("aa", "ba"), check_vma=False
    )
```

```python
import functools

import jax
import jax.numpy as jnp
from jax import lax
from jax.experimental import pallas as pl
from jax.experimental.pallas import tpu as pltpu
from jax.sharding import PartitionSpec as P

BF16 = jnp.bfloat16
F32 = jnp.float32
I32 = jnp.int32
RESIDENT = 8 * 2**20
VMEM_LIMIT = 48 * 2**20


def iota(shape, dim):
    return lax.broadcasted_iota(I32, shape, dim)


def dot(x, y):
    return jnp.dot(x, y, preferred_element_type=F32)


def dot_nt(x, y):
    return lax.dot_general(x, y, (((1,), (1,)), ((), ())), preferred_element_type=F32)


def live_ids(counts_ref, first, shape, dim, cap):
    ids = iota(shape, dim)
    block = ids // cap
    count = jnp.zeros(shape, I32)
    for j in range(shape[dim] // cap):
        count = jnp.where(block == j, counts_ref[first // cap + j], count)
    return jnp.where(ids - block * cap < count, ids + first + 1, -1)


def sign_of(code):
    return jnp.where(code > 0, 1.0, -1.0).astype(F32)


def mix_kernel(steps, cap, place, counts_hbm, irrep_hbm, code_hbm, integrals_hbm, gains_hbm, amplitudes_hbm, *refs):
    mixed_ref, one_ref, code_ref, ids_ref, alive_ref, amplitudes_ref = refs[:6]
    counts_ref, irrep_ref, integrals_ref, gains_ref, sems = refs[6:]
    pairs, strings = code_ref.shape
    tile = one_ref.shape[0]
    rows, columns = amplitudes_ref.shape
    step = 0 if steps == 1 else pl.program_id(0)
    group, first_a, first_b = place()
    copies = [
        pltpu.make_async_copy(source, target, sems.at[i])
        for i, (source, target) in enumerate(
            (
                (counts_hbm, counts_ref),
                (irrep_hbm, irrep_ref),
                (code_hbm, code_ref),
                (integrals_hbm, integrals_ref),
                (gains_hbm, gains_ref),
                (amplitudes_hbm, amplitudes_ref),
            )
        )
    ]
    for copy in copies:
        copy.start()
    wide = pairs * 8
    spread_q = jnp.where(iota((wide, pairs), 0) // 8 == iota((wide, pairs), 1), 1.0, 0.0).astype(BF16)
    spread_p = jnp.where(iota((pairs, wide), 1) % pairs == iota((pairs, wide), 0), 1.0, 0.0).astype(BF16)
    for copy in copies:
        copy.wait()
    ids = live_ids(counts_ref, 0, (1, strings), 1, cap)
    ids_ref[...] = live_ids(counts_ref, first_b, ids_ref.shape, 0, cap)
    live_a = live_ids(counts_ref, first_a, (rows, columns), 0, cap)
    live_b = live_ids(counts_ref, first_b, (1, columns), 1, cap)
    alive_ref[...] = jnp.where((live_a > 0) & (live_b > 0), 1.0, 0.0)
    irrep_p = jnp.zeros((pairs, pairs), I32)
    irrep_q = jnp.zeros((pairs, pairs), I32)
    for p in range(pairs):
        irrep_p = jnp.where(iota((pairs, pairs), 0) == p, irrep_ref[p], irrep_p)
        irrep_q = jnp.where(iota((pairs, pairs), 1) == p, irrep_ref[p], irrep_q)
    weights = jnp.where(irrep_p == irrep_q, integrals_ref[...].astype(F32), 0.0).astype(BF16)
    left = jnp.concatenate(
        [dot_nt(spread_q, weights), jnp.broadcast_to(gains_ref[...].astype(F32), (8, pairs))], 0
    ).astype(BF16)
    mixer = dot(left, spread_p)
    same = iota(mixer.shape, 0) % 8 == iota(mixer.shape, 1) // pairs
    mixer = jnp.where(same, mixer, 0.0).astype(BF16)
    code = code_ref[:, pl.ds(pl.multiple_of(group * 2 * rows + step * tile, 128), tile)]
    size = jnp.abs(code)
    sign = sign_of(code)
    for base in range(0, tile, 16):
        halves = []
        for low in (base, base + 8):
            hot = jnp.concatenate(
                [
                    jnp.where(size[:, a : a + 1] == ids, sign[:, a : a + 1], 0.0).astype(BF16)
                    for a in range(low, low + 8)
                ],
                0,
            )
            part = dot(mixer, hot)
            one_ref[pl.ds(low, 8), :] = part[wide:]
            halves.append(part[:wide].reshape(pairs, 8, strings))
        mixed_ref[:, pl.ds(base, 16), :] = jnp.concatenate(halves, 1).astype(BF16)


def same_spin_kernel(steps, place, ids_ref, code_ref, mixed_ref, one_ref, own_ref, sibling_ref, hot_ref, message_ref, total_ref):
    pairs, chip, strings = mixed_ref.shape
    rows, columns = own_ref.shape
    step = 0 if steps == 1 else pl.program_id(0)
    core, first_b = place()
    ids = jnp.concatenate([ids_ref[...]] * (strings // 128), 1)

    @pl.when(step == 0)
    def _():
        total_ref[...] = jnp.zeros_like(total_ref)

    total = total_ref[...]
    for q in range(pairs):
        code = code_ref[q : q + 1, :]
        hot = jnp.where(jnp.abs(code) == ids, sign_of(code), 0.0).astype(BF16)
        hot_ref[pl.ds(q * columns, columns), :] = hot
        total = total + dot_nt(mixed_ref[q], hot)
    total_ref[...] = total

    @pl.when(step == steps - 1)
    def _():
        message_ref[pl.ds(pl.multiple_of(core * rows, rows), rows), :] = own_ref[...]
        message_ref[pl.ds(pl.multiple_of((1 - core) * rows, rows), rows), :] = sibling_ref[...]
        one = one_ref[:, pl.ds(pl.multiple_of(first_b, 128), columns)]
        message_ref[chip:] = (one + 0.5 * total_ref[...]).astype(BF16)


def mixed_kernel(steps, groups, peers, place, mixed_ref, hot_ref, *refs):
    arrived = refs[:groups]
    own_ref, amplitudes_ref = refs[groups : groups + 2]
    sent = refs[groups + 2 : groups + 1 + peers]
    all_f, line, total_ref = refs[groups + 1 + peers :]
    pairs, rows, strings = mixed_ref.shape[0], own_ref.shape[0], mixed_ref.shape[2]
    columns = own_ref.shape[1]
    chip = 2 * rows
    step = 0 if steps == 1 else pl.program_id(0)
    group, core, column = place()

    @pl.when(step == 0)
    def _():
        for k in range(groups):
            at = pl.multiple_of((group ^ k) * chip, chip)
            amplitudes_ref[pl.ds(at, chip), :] = arrived[k][:chip]
            all_f[pl.ds(at, chip), :] = arrived[k][chip:]
        at = pl.multiple_of(core * rows, rows)
        total_ref[...] = dot_nt(arrived[0][pl.ds(at, rows), :], all_f[...])

    amplitudes = amplitudes_ref[...]
    at = pl.multiple_of(core * rows, rows) if mixed_ref.shape[1] != rows else 0
    for q in range(pairs):
        part = dot(mixed_ref[q, pl.ds(at, rows), :], amplitudes)
        line[:, pl.ds(q * columns, columns)] = part.astype(BF16)
    total_ref[...] += dot(line[...], hot_ref[...])

    @pl.when(step == steps - 1)
    def _():
        own_f = arrived[0][pl.ds(pl.multiple_of(chip + core * rows, rows), rows), :]
        for k in range(peers):
            part = total_ref[:, pl.ds(pl.multiple_of((column ^ k) * columns, columns), columns)]
            if k == 0:
                own_ref[...] = part
            else:
                sent[k - 1][:rows] = part.astype(BF16)
                sent[k - 1][rows:] = own_f


def final_kernel(peers, place, alive_ref, own_ref, amplitudes_ref, message_ref, *refs):
    arrived, out_ref = refs[:-1], refs[-1]
    rows, columns = own_ref.shape
    core, column = place()
    total = own_ref[...]
    own_f = message_ref[pl.ds(pl.multiple_of((2 + core) * rows, rows), rows), :]
    for k in range(peers):
        block = amplitudes_ref[pl.ds(pl.multiple_of((column ^ k) * columns, columns), columns), :]
        if k == 0:
            total = total + dot(own_f, block)
        else:
            total = total + arrived[k - 1][:rows].astype(F32) + dot(arrived[k - 1][rows:], block)
    out_ref[...] = (total * alive_ref[...]).astype(BF16)


def per_device(sizes, amplitudes, code, counts, pair_irrep, integrals, one_body):
    rows, columns = amplitudes.shape
    pairs, strings = code.shape
    cap = strings // counts.shape[0]
    groups, peers = sizes[0] // 2, sizes[1]
    chip = 2 * rows
    resident = pairs * chip * strings * 2 <= RESIDENT
    row_tiles = 1 if resident else chip // 128
    pair_tiles = 1 if resident else pairs // 4
    tile, part = chip // row_tiles, pairs // pair_tiles
    hbm = pl.BlockSpec(memory_space=pl.ANY)
    vmem = pl.BlockSpec(memory_space=pltpu.VMEM)

    def tiled(shape, dim):
        if resident:
            return vmem
        return pl.BlockSpec(shape, lambda i: tuple(i if d == dim else 0 for d in range(len(shape))))

    def shape_of(shape, dtype):
        return pltpu.VMEM(shape, dtype) if resident else jax.ShapeDtypeStruct(shape, dtype)

    def near(value):
        return pltpu.with_memory_space_constraint(value, pltpu.VMEM) if resident else value

    def far(value):
        return pltpu.with_memory_space_constraint(value, pltpu.HBM)

    def call(body, name, tiles, *args, **keys):
        if tiles > 1:
            keys["grid"] = (tiles,)
        params = pltpu.CompilerParams(vmem_limit_bytes=VMEM_LIMIT)
        return pl.pallas_call(body, name=name, compiler_params=params, **keys)(*args)

    def send(value, axis, mask):
        return lax.ppermute(value, axis, [(i, i ^ mask) for i in range(lax.axis_size(axis))])

    def alpha():
        return lax.axis_index("aa")

    def beta():
        return lax.axis_index("ba")

    sibling = send(amplitudes, "aa", 1)
    mixed, one, codes, ids, alive, own_c = call(
        functools.partial(mix_kernel, row_tiles, cap, lambda: (alpha() // 2, alpha() * rows, beta() * columns)),
        "mix",
        row_tiles,
        far(counts),
        far(pair_irrep),
        far(code),
        far(integrals),
        far(one_body.reshape(1, pairs)),
        far(amplitudes),
        in_specs=[hbm] * 6,
        out_shape=(
            shape_of((pairs, chip, strings), BF16),
            shape_of((chip, strings), F32),
            shape_of((pairs, strings), I32),
            shape_of((columns, 128), I32),
            shape_of((rows, columns), F32),
            shape_of((rows, columns), BF16),
        ),
        out_specs=(tiled((pairs, tile, strings), 1), tiled((tile, strings), 0), vmem, vmem, vmem, vmem),
        scratch_shapes=[
            pltpu.SMEM(counts.shape, I32),
            pltpu.SMEM(pair_irrep.shape, I32),
            pltpu.VMEM((pairs, pairs), BF16),
            pltpu.VMEM((1, pairs), BF16),
            pltpu.SemaphoreType.DMA((6,)),
        ],
    )
    hot, message = call(
        functools.partial(same_spin_kernel, pair_tiles, lambda: (alpha() % 2, beta() * columns)),
        "same_spin",
        pair_tiles,
        near(ids),
        near(codes) if resident else codes.reshape(pair_tiles, part, strings),
        near(mixed),
        near(one),
        near(own_c),
        near(sibling),
        in_specs=[
            vmem,
            vmem if resident else pl.BlockSpec((None, part, strings), lambda i: (i, 0, 0)),
            tiled((part, chip, strings), 0),
            vmem,
            vmem,
            vmem,
        ],
        out_shape=(shape_of((pairs * columns, strings), BF16), shape_of((2 * chip, columns), BF16)),
        out_specs=(tiled((part * columns, strings), 0), vmem),
        scratch_shapes=[pltpu.VMEM((chip, columns), F32)],
    )
    messages = [message] + [send(message, "aa", 2 * k) for k in range(1, groups)]
    outs = call(
        functools.partial(mixed_kernel, pair_tiles, groups, peers, lambda: (alpha() // 2, alpha() % 2, beta())),
        "mixed",
        pair_tiles,
        near(mixed),
        near(hot),
        *[near(m) for m in messages],
        in_specs=[tiled((part, chip, strings), 0), tiled((part * columns, strings), 0)] + [vmem] * groups,
        out_shape=(shape_of((rows, columns), F32), shape_of((strings, columns), BF16))
        + tuple(shape_of((2 * rows, columns), BF16) for _ in range(peers - 1)),
        out_specs=(vmem,) * (peers + 1),
        scratch_shapes=[
            pltpu.VMEM((strings, columns), BF16),
            pltpu.VMEM((rows, part * columns), BF16),
            pltpu.VMEM((rows, strings), F32),
        ],
    )
    own, gathered = outs[:2]
    arrived = [send(m, "ba", k + 1) for k, m in enumerate(outs[2:])]
    return call(
        functools.partial(final_kernel, peers, lambda: (alpha() % 2, beta())),
        "final",
        1,
        near(alive),
        near(own),
        near(gathered),
        near(message),
        *[near(m) for m in arrived],
        in_specs=[vmem] * (3 + peers),
        out_shape=jax.ShapeDtypeStruct((rows, columns), BF16),
        out_specs=vmem,
    )


def solution(mesh):
    placed = (P("aa", "ba"), P(), P(), P(), P(), P())
    sizes = (mesh.shape["aa"], mesh.shape["ba"])
    return jax.shard_map(
        functools.partial(per_device, sizes), mesh=mesh, in_specs=placed, out_specs=P("aa", "ba"), check_vma=False
    )
```

```python
import functools

import jax
import jax.numpy as jnp
from jax import lax
from jax.experimental import pallas as pl
from jax.experimental.pallas import tpu as pltpu
from jax.sharding import PartitionSpec as P

BF16 = jnp.bfloat16
F32 = jnp.float32
I32 = jnp.int32
I16 = jnp.int16
RESIDENT = 8 * 2**20
VMEM_LIMIT = 48 * 2**20
NEAR_LIMIT = 16 * 2**20
SIDE_PIECES = 2


def iota(shape, dim):
    return lax.broadcasted_iota(I32, shape, dim)


def dot(x, y):
    return jnp.dot(x, y, preferred_element_type=F32)


def dot_nt(x, y):
    return lax.dot_general(x, y, (((1,), (1,)), ((), ())), preferred_element_type=F32)


def live_ids(counts_ref, first, shape, dim, cap):
    ids = iota(shape, dim)
    block = ids // cap
    count = jnp.zeros(shape, I32)
    for j in range(shape[dim] // cap):
        count = jnp.where(block == j, counts_ref[first // cap + j], count)
    return jnp.where(ids - block * cap < count, ids + first + 1, -1)


def sign_of(code):
    return jnp.where(code > 0, 1.0, -1.0).astype(F32)


def tables_kernel(cap, place, counts_hbm, irrep_hbm, code_hbm, integrals_hbm, gains_hbm, amplitudes_hbm, *refs):
    code_ref, live_ref, mixer_ref, alive_ref, amplitudes_ref = refs[:5]
    counts_ref, irrep_ref, integrals_ref, gains_ref, sems = refs[5:]
    pairs, strings = code_ref.shape
    rows, columns = amplitudes_ref.shape
    first_a, first_b = place()
    copies = [
        pltpu.make_async_copy(source, target, sems.at[i])
        for i, (source, target) in enumerate(
            (
                (irrep_hbm, irrep_ref),
                (integrals_hbm, integrals_ref),
                (gains_hbm, gains_ref),
                (counts_hbm, counts_ref),
                (code_hbm, code_ref),
                (amplitudes_hbm, amplitudes_ref),
            )
        )
    ]
    for copy in copies:
        copy.start()
    wide = pairs * 8
    spread_q = jnp.where(iota((wide, pairs), 0) // 8 == iota((wide, pairs), 1), 1.0, 0.0).astype(BF16)
    spread_p = jnp.where(iota((pairs, wide), 1) % pairs == iota((pairs, wide), 0), 1.0, 0.0).astype(BF16)
    for copy in copies:
        copy.wait()
    irrep_p = jnp.zeros((pairs, pairs), I32)
    irrep_q = jnp.zeros((pairs, pairs), I32)
    for p in range(pairs):
        irrep_p = jnp.where(iota((pairs, pairs), 0) == p, irrep_ref[p], irrep_p)
        irrep_q = jnp.where(iota((pairs, pairs), 1) == p, irrep_ref[p], irrep_q)
    weights = jnp.where(irrep_p == irrep_q, integrals_ref[...].astype(F32), 0.0).astype(BF16)
    left = jnp.concatenate(
        [dot_nt(spread_q, weights), jnp.broadcast_to(gains_ref[...].astype(F32), (8, pairs))], 0
    ).astype(BF16)
    mixer = dot(left, spread_p)
    same = iota(mixer.shape, 0) % 8 == iota(mixer.shape, 1) // pairs
    mixer_ref[...] = jnp.where(same, mixer, 0.0).astype(BF16)
    live_ref[...] = live_ids(counts_ref, 0, live_ref.shape, 0, cap)
    live_a = live_ids(counts_ref, first_a, (rows, columns), 0, cap)
    live_b = live_ids(counts_ref, first_b, (1, columns), 1, cap)
    alive_ref[...] = jnp.where((live_a > 0) & (live_b > 0), 1.0, 0.0)


def join_kernel(own_ref, sibling_ref, message_ref):
    rows = own_ref.shape[0]
    message_ref[:rows] = own_ref[...]
    message_ref[rows:] = sibling_ref[...]


def mix_kernel(columns_at, code_ref, live_ref, mixer_ref, after_ref, mixed_ref, one_ref):
    pairs, strings = code_ref.shape
    wide = pairs * 8
    ids = jnp.broadcast_to(jnp.transpose(live_ref[...])[:1], (pairs, strings)).astype(I16)
    zero = jnp.zeros(ids.shape, BF16)
    mixer = mixer_ref[...]
    code = columns_at(code_ref)
    size = jnp.abs(code)
    sign = sign_of(code)
    for base in range(0, code.shape[1], 16):
        halves = []
        for low in (base, base + 8):
            hot = jnp.concatenate(
                [
                    jnp.where(
                        jnp.broadcast_to(size[:, a : a + 1], ids.shape).astype(I16) == ids,
                        jnp.broadcast_to(sign[:, a : a + 1], ids.shape).astype(BF16),
                        zero,
                    )
                    for a in range(low, low + 8)
                ],
                0,
            )
            part = dot(mixer, hot)
            one_ref[pl.ds(low, 8), :] = part[wide:]
            halves.append(part[:wide].reshape(pairs, 8, strings))
        mixed_ref[:, pl.ds(base, 16), :] = jnp.concatenate(halves, 1).astype(BF16)


def hot_tile(code, ids):
    size = jnp.broadcast_to(jnp.abs(code), ids.shape).astype(I16)
    sign = jnp.broadcast_to(sign_of(code), ids.shape).astype(BF16)
    return jnp.where(size == ids, sign, jnp.zeros(ids.shape, BF16))


def row_ids(live_ref, first, rows, strings):
    return jnp.concatenate([live_ref[pl.ds(first, rows), :]] * (strings // 128), 1).astype(I16)


def hot_kernel(steps, place, live_ref, code_ref, mixed_ref, one_ref, hot_ref, block_ref, total_ref):
    pairs, strings = code_ref.shape
    rows, columns = block_ref.shape
    step = 0 if steps == 1 else pl.program_id(0)
    first = pl.multiple_of(place(), columns)
    ids = row_ids(live_ref, first, columns, strings)
    if steps > 1:

        @pl.when(step == 0)
        def _():
            total_ref[...] = jnp.zeros_like(total_ref)

    total = jnp.zeros((rows, columns), F32) if steps == 1 else total_ref[...]
    for q in range(pairs):
        hot = hot_tile(code_ref[q : q + 1, :], ids)
        hot_ref[pl.ds(q * columns, columns), :] = hot
        total = total + dot_nt(mixed_ref[q, :rows, :], hot)
    if steps > 1:
        total_ref[...] = total
    block_ref[...] = (one_ref[:rows, pl.ds(first, columns)] + 0.5 * total).astype(BF16)


def mixed_kernel(steps, groups, peers, place, mixed_ref, hot_ref, block_ref, *refs):
    arrived = refs[:groups]
    own_ref, amplitudes_ref = refs[groups : groups + 2]
    sent = refs[groups + 2 : groups + 1 + peers]
    line, total_ref = refs[groups + 1 + peers :]
    pairs, strings = mixed_ref.shape[0], mixed_ref.shape[2]
    rows, columns = own_ref.shape
    step = 0 if steps == 1 else pl.program_id(0)
    group, core, column = place()

    @pl.when(step == 0)
    def _():
        total_ref[...] = jnp.zeros_like(total_ref)
        for k in range(groups):
            first = (group ^ k) * 2
            at = pl.multiple_of((first + core) * rows, rows)
            amplitudes_ref[pl.ds(at, rows), :] = arrived[k][:rows]
            at = pl.multiple_of((first + 1 - core) * rows, rows)
            amplitudes_ref[pl.ds(at, rows), :] = arrived[k][rows:]

    amplitudes = amplitudes_ref[...]
    for q in range(pairs):
        part = dot(mixed_ref[q, :rows, :], amplitudes)
        line[:, pl.ds(q * columns, columns)] = part.astype(BF16)
    total_ref[...] += dot(line[...], hot_ref[...])

    @pl.when(step == steps - 1)
    def _():
        for k in range(peers):
            to = lax.rem(column + k, peers)
            part = total_ref[:, pl.ds(pl.multiple_of(to * columns, columns), columns)]
            if k == 0:
                own_ref[...] = part
            else:
                sent[k - 1][:rows] = part.astype(BF16)
                sent[k - 1][rows : 2 * rows] = arrived[0][:rows]
                sent[k - 1][2 * rows :] = block_ref[...]


def same_spin_kernel(steps, place, live_ref, code_ref, mixed_ref, one_ref, after_ref, *refs):
    pairs, both, strings = mixed_ref.shape
    side_refs, total_ref = refs[:-1], refs[-1]
    piece, columns = side_refs[0].shape
    half = piece * len(side_refs)
    step = 0 if steps == 1 else pl.program_id(0)
    at = pl.multiple_of(place() * half, half)
    tile = piece
    if steps > 1:

        @pl.when(step == 0)
        def _():
            total_ref[...] = jnp.zeros_like(total_ref)

    for first in range(0, half, tile):
        ids = row_ids(live_ref, at + first, tile, strings)
        total = jnp.zeros((tile, columns), F32) if steps == 1 else total_ref[pl.ds(first, tile), :]
        for q in range(pairs):
            total = total + dot_nt(hot_tile(code_ref[q : q + 1, :], ids), mixed_ref[q, both - columns :, :])
        if steps > 1:
            total_ref[pl.ds(first, tile), :] = total
        one = jnp.transpose(one_ref[both - columns :, pl.ds(at + first, tile)])
        side_refs[first // piece][...] = (one + 0.5 * total).astype(BF16)


def final_kernel(peers, place, alive_ref, own_ref, amplitudes_ref, message_ref, block_ref, *refs):
    out_ref, side_ref = refs[-2:]
    arrived, sides = refs[: peers - 1], refs[peers - 1 : -2]
    rows, columns = own_ref.shape
    piece = sides[0].shape[0]
    pieces = len(sides) // 2
    core, column = place()
    for i in range(pieces):
        side_ref[pl.ds(pl.multiple_of((core * pieces + i) * piece, piece), piece), :] = sides[i][...]
        at = pl.multiple_of(((1 - core) * pieces + i) * piece, piece)
        side_ref[pl.ds(at, piece), :] = sides[pieces + i][...]
    total = own_ref[...]
    left, right = [], []
    for k in range(peers):
        source = lax.rem(column + peers - k, peers)
        at = pl.multiple_of(source * columns, columns)
        if k == 0:
            left += [block_ref[...], message_ref[:rows]]
        else:
            left += [arrived[k - 1][2 * rows :], arrived[k - 1][rows : 2 * rows]]
            total = total + arrived[k - 1][:rows].astype(F32)
        right += [amplitudes_ref[pl.ds(at, columns), :], side_ref[pl.ds(at, columns), :]]
    total = total + dot(jnp.concatenate(left, 1), jnp.concatenate(right, 0))
    out_ref[...] = (total * alive_ref[...]).astype(BF16)


def per_device(sizes, amplitudes, code, counts, pair_irrep, integrals, one_body):
    rows, columns = amplitudes.shape
    pairs, strings = code.shape
    cap = strings // counts.shape[0]
    groups, peers = sizes[0] // 2, sizes[1]
    both = rows + columns
    resident = pairs * both * strings * 2 <= RESIDENT
    tile = both if resident else 128
    row_tiles = both // tile
    pair_tiles = 1 if resident else pairs // 4
    part = pairs // pair_tiles
    hbm = pl.BlockSpec(memory_space=pl.ANY)
    vmem = pl.BlockSpec(memory_space=pltpu.VMEM)

    def tiled(shape, dim):
        if resident:
            return vmem
        return pl.BlockSpec(shape, lambda i: tuple(i if d == dim else 0 for d in range(len(shape))))

    def shape_of(shape, dtype):
        return pltpu.VMEM(shape, dtype) if resident else jax.ShapeDtypeStruct(shape, dtype)

    def near(value):
        return pltpu.with_memory_space_constraint(value, pltpu.VMEM) if resident else value

    def far(value):
        return pltpu.with_memory_space_constraint(value, pltpu.HBM)

    def call(body, name, tiles, *args, flops=0, **keys):
        if tiles > 1:
            keys["grid"] = (tiles,)
        params = pltpu.CompilerParams(vmem_limit_bytes=NEAR_LIMIT if resident else VMEM_LIMIT)
        cost = pl.CostEstimate(flops=flops, bytes_accessed=0, transcendentals=0)
        return pl.pallas_call(body, name=name, compiler_params=params, cost_estimate=cost, **keys)(*args)

    def alpha():
        return lax.axis_index("aa")

    def beta():
        return lax.axis_index("ba")

    def over_alpha(value, mask):
        return lax.ppermute(value, "aa", [(i, i ^ mask) for i in range(sizes[0])])

    def over_beta(value, shift):
        return lax.ppermute(value, "ba", [(i, (i + shift) % peers) for i in range(peers)])

    def columns_at(code_ref):
        if resident:
            chip = code_ref[:, pl.ds(pl.multiple_of(alpha() // 2 * 2 * rows, 2 * rows), 2 * rows)]
            own = jnp.where(alpha() % 2 == 0, chip[:, :rows], chip[:, rows:])
            return jnp.concatenate([own, code_ref[:, pl.ds(pl.multiple_of(beta() * columns, columns), columns)]], 1)
        at = pl.program_id(0) * tile
        first = jnp.where(at < rows, alpha() * rows + at, beta() * columns + at - rows)
        return code_ref[:, pl.ds(pl.multiple_of(first, tile), tile)]

    sibling = over_alpha(amplitudes, 1)
    codes, live, mixer, alive, own_c = call(
        functools.partial(tables_kernel, cap, lambda: (alpha() * rows, beta() * columns)),
        "tables",
        1,
        far(counts),
        far(pair_irrep),
        far(code),
        far(integrals),
        far(one_body.reshape(1, pairs)),
        far(amplitudes),
        in_specs=[hbm] * 6,
        out_shape=(
            shape_of((pairs, strings), I32),
            shape_of((strings, 128), I32),
            shape_of((pairs * 8 + 8, pairs * 8), BF16),
            shape_of((rows, columns), F32),
            shape_of((rows, columns), BF16),
        ),
        out_specs=(vmem,) * 5,
        scratch_shapes=[
            pltpu.SMEM(counts.shape, I32),
            pltpu.SMEM(pair_irrep.shape, I32),
            pltpu.VMEM((pairs, pairs), BF16),
            pltpu.VMEM((1, pairs), BF16),
            pltpu.SemaphoreType.DMA((6,)),
        ],
    )
    message = call(
        join_kernel,
        "join",
        1,
        near(own_c),
        near(sibling),
        in_specs=[vmem] * 2,
        out_shape=shape_of((2 * rows, columns), BF16),
        out_specs=vmem,
    )
    messages = [message] + [over_alpha(message, 2 * k) for k in range(1, groups)]
    mixed, one = call(
        functools.partial(mix_kernel, columns_at),
        "mix",
        row_tiles,
        near(codes),
        near(live),
        near(mixer),
        near(message),
        flops=2 * both * pairs * pairs * 8 * strings,
        in_specs=[vmem] * 4,
        out_shape=(shape_of((pairs, both, strings), BF16), shape_of((both, strings), F32)),
        out_specs=(tiled((pairs, tile, strings), 1), tiled((tile, strings), 0)),
    )
    code_parts = near(codes) if resident else codes.reshape(pair_tiles, part, strings)
    code_spec = vmem if resident else pl.BlockSpec((None, part, strings), lambda i: (i, 0, 0))
    hot, block = call(
        functools.partial(hot_kernel, pair_tiles, lambda: beta() * columns),
        "hot",
        pair_tiles,
        near(live),
        code_parts,
        near(mixed),
        near(one),
        flops=2 * pairs * rows * columns * strings,
        in_specs=[vmem, code_spec, tiled((part, both, strings), 0), vmem],
        out_shape=(shape_of((pairs * columns, strings), BF16), shape_of((rows, columns), BF16)),
        out_specs=(tiled((part * columns, strings), 0), vmem),
        scratch_shapes=[pltpu.VMEM((rows, columns), F32)],
    )
    outs = call(
        functools.partial(mixed_kernel, pair_tiles, groups, peers, lambda: (alpha() // 2, alpha() % 2, beta())),
        "mixed",
        pair_tiles,
        near(mixed),
        near(hot),
        near(block),
        *[near(m) for m in messages],
        in_specs=[tiled((part, both, strings), 0), tiled((part * columns, strings), 0)] + [vmem] * (groups + 1),
        out_shape=(shape_of((rows, columns), F32), shape_of((strings, columns), BF16))
        + tuple(shape_of((3 * rows, columns), BF16) for _ in range(peers - 1)),
        out_specs=(vmem,) * (peers + 1),
        scratch_shapes=[pltpu.VMEM((rows, part * columns), BF16), pltpu.VMEM((rows, strings), F32)],
    )
    own, gathered = outs[:2]
    arrived = [over_beta(m, k + 1) for k, m in enumerate(outs[2:])]
    pieces = SIDE_PIECES
    sides = call(
        functools.partial(same_spin_kernel, pair_tiles, lambda: alpha() % 2),
        "same_spin",
        pair_tiles,
        near(live),
        code_parts,
        near(mixed),
        near(one),
        near(own),
        flops=2 * columns * pairs * strings * strings,
        in_specs=[vmem, code_spec, tiled((part, both, strings), 0)] + [vmem] * 2,
        out_shape=tuple(shape_of((strings // 2 // pieces, columns), BF16) for _ in range(pieces)),
        out_specs=(vmem,) * pieces,
        scratch_shapes=[pltpu.VMEM((strings // 2, columns), F32)],
    )
    sides = list(sides) + [over_alpha(side, 1) for side in sides]
    return call(
        functools.partial(final_kernel, peers, lambda: (alpha() % 2, beta())),
        "final",
        1,
        near(alive),
        near(own),
        near(gathered),
        near(message),
        near(block),
        *[near(m) for m in arrived],
        *[near(side) for side in sides],
        in_specs=[vmem] * (4 + peers + 2 * pieces),
        out_shape=jax.ShapeDtypeStruct((rows, columns), BF16),
        out_specs=vmem,
        scratch_shapes=[pltpu.VMEM((strings, columns), BF16)],
    )


def solution(mesh):
    placed = (P("aa", "ba"), P(), P(), P(), P(), P())
    sizes = (mesh.shape["aa"], mesh.shape["ba"])
    return jax.shard_map(
        functools.partial(per_device, sizes), mesh=mesh, in_specs=placed, out_specs=P("aa", "ba"), check_vma=False
    )
```

```python
import functools

import jax
import jax.numpy as jnp
from jax import lax
from jax.experimental import pallas as pl
from jax.experimental.pallas import tpu as pltpu
from jax.sharding import PartitionSpec as P

BF16 = jnp.bfloat16
F32 = jnp.float32
I32 = jnp.int32
I16 = jnp.int16
RESIDENT = 8 * 2**20
VMEM_LIMIT = 48 * 2**20
NEAR_LIMIT = 16 * 2**20
SIDE_PIECES = 2


def iota(shape, dim):
    return lax.broadcasted_iota(I32, shape, dim)


def dot(x, y):
    return jnp.dot(x, y, preferred_element_type=F32)


def dot_nt(x, y):
    return lax.dot_general(x, y, (((1,), (1,)), ((), ())), preferred_element_type=F32)


def live_ids(counts_ref, first, shape, dim, cap):
    ids = iota(shape, dim)
    block = ids // cap
    count = jnp.zeros(shape, I32)
    for j in range(shape[dim] // cap):
        count = jnp.where(block == j, counts_ref[first // cap + j], count)
    return jnp.where(ids - block * cap < count, ids + first + 1, -1)


def sign_of(code):
    return jnp.where(code > 0, 1.0, -1.0).astype(F32)


def tables_kernel(cap, place, counts_hbm, irrep_hbm, code_hbm, integrals_hbm, gains_hbm, amplitudes_hbm, *refs):
    code_ref, live_ref, mixer_ref, alive_ref, amplitudes_ref = refs[:5]
    counts_ref, irrep_ref, integrals_ref, gains_ref, sems = refs[5:]
    pairs, strings = code_ref.shape
    rows, columns = amplitudes_ref.shape
    first_a, first_b = place()
    copies = [
        pltpu.make_async_copy(source, target, sems.at[i])
        for i, (source, target) in enumerate(
            (
                (irrep_hbm, irrep_ref),
                (integrals_hbm, integrals_ref),
                (gains_hbm, gains_ref),
                (counts_hbm, counts_ref),
                (code_hbm, code_ref),
                (amplitudes_hbm, amplitudes_ref),
            )
        )
    ]
    for copy in copies:
        copy.start()
    wide = pairs * 8
    spread_q = jnp.where(iota((wide, pairs), 0) // 8 == iota((wide, pairs), 1), 1.0, 0.0).astype(BF16)
    spread_p = jnp.where(iota((pairs, wide), 1) % pairs == iota((pairs, wide), 0), 1.0, 0.0).astype(BF16)
    for copy in copies:
        copy.wait()
    irrep_p = jnp.zeros((pairs, pairs), I32)
    irrep_q = jnp.zeros((pairs, pairs), I32)
    for p in range(pairs):
        irrep_p = jnp.where(iota((pairs, pairs), 0) == p, irrep_ref[p], irrep_p)
        irrep_q = jnp.where(iota((pairs, pairs), 1) == p, irrep_ref[p], irrep_q)
    weights = jnp.where(irrep_p == irrep_q, integrals_ref[...].astype(F32), 0.0).astype(BF16)
    left = jnp.concatenate(
        [dot_nt(spread_q, weights), jnp.broadcast_to(gains_ref[...].astype(F32), (8, pairs))], 0
    ).astype(BF16)
    mixer = dot(left, spread_p)
    same = iota(mixer.shape, 0) % 8 == iota(mixer.shape, 1) // pairs
    mixer_ref[...] = jnp.where(same, mixer, 0.0).astype(BF16)
    live_ref[...] = live_ids(counts_ref, 0, live_ref.shape, 0, cap)
    live_a = live_ids(counts_ref, first_a, (rows, columns), 0, cap)
    live_b = live_ids(counts_ref, first_b, (1, columns), 1, cap)
    alive_ref[...] = jnp.where((live_a > 0) & (live_b > 0), 1.0, 0.0)


def join_kernel(own_ref, sibling_ref, message_ref):
    rows = own_ref.shape[0]
    message_ref[:rows] = own_ref[...]
    message_ref[rows:] = sibling_ref[...]


def mix_kernel(columns_at, code_ref, live_ref, mixer_ref, after_ref, mixed_ref, one_ref):
    pairs, strings = code_ref.shape
    wide = pairs * 8
    ids = jnp.broadcast_to(jnp.transpose(live_ref[...])[:1], (pairs, strings)).astype(I16)
    zero = jnp.zeros(ids.shape, BF16)
    mixer = mixer_ref[...]
    code = columns_at(code_ref)
    size = jnp.abs(code)
    sign = sign_of(code)

    def along(table, at, dtype):
        tile = jnp.broadcast_to(table[:, at : at + 1], (pairs, 128)).astype(dtype)
        return jnp.concatenate([tile] * (strings // 128), 1)

    for base in range(0, code.shape[1], 16):
        halves = []
        for low in (base, base + 8):
            hot = jnp.concatenate(
                [
                    jnp.where(along(size, a, I16) == ids, along(sign, a, BF16), zero)
                    for a in range(low, low + 8)
                ],
                0,
            )
            part = dot(mixer, hot)
            one_ref[pl.ds(low, 8), :] = part[wide:]
            halves.append(part[:wide].reshape(pairs, 8, strings))
        mixed_ref[:, pl.ds(base, 16), :] = jnp.concatenate(halves, 1).astype(BF16)


def hot_tile(code, ids):
    rows, strings = ids.shape
    size = jnp.broadcast_to(jnp.abs(code), (16, strings)).astype(I16)
    sign = jnp.broadcast_to(sign_of(code), (16, strings)).astype(BF16)
    size = jnp.concatenate([size] * (rows // 16), 0)
    sign = jnp.concatenate([sign] * (rows // 16), 0)
    return jnp.where(size == ids, sign, jnp.zeros(ids.shape, BF16))


def row_ids(live_ref, first, rows, strings):
    return jnp.concatenate([live_ref[pl.ds(first, rows), :]] * (strings // 128), 1).astype(I16)


def hot_kernel(steps, place, live_ref, code_ref, mixed_ref, one_ref, hot_ref, block_ref, total_ref):
    pairs, strings = code_ref.shape
    rows, columns = block_ref.shape
    step = 0 if steps == 1 else pl.program_id(0)
    first = pl.multiple_of(place(), columns)
    ids = row_ids(live_ref, first, columns, strings)
    if steps > 1:

        @pl.when(step == 0)
        def _():
            total_ref[...] = jnp.zeros_like(total_ref)

    total = jnp.zeros((columns, rows), F32) if steps == 1 else total_ref[...]
    for q in range(pairs):
        hot = hot_tile(code_ref[q : q + 1, :], ids)
        hot_ref[pl.ds(q * columns, columns), :] = hot
        total = total + dot_nt(hot, mixed_ref[q, :rows, :])
    if steps > 1:
        total_ref[...] = total
    block_ref[...] = (one_ref[:rows, pl.ds(first, columns)] + 0.5 * jnp.transpose(total)).astype(BF16)


def mixed_kernel(steps, groups, peers, place, mixed_ref, hot_ref, block_ref, *refs):
    arrived = refs[:groups]
    own_ref, amplitudes_ref = refs[groups : groups + 2]
    sent = refs[groups + 2 : groups + 1 + peers][::-1]
    line, total_ref = refs[groups + 1 + peers :]
    pairs, strings = mixed_ref.shape[0], mixed_ref.shape[2]
    rows, columns = own_ref.shape
    step = 0 if steps == 1 else pl.program_id(0)
    group, core, column = place()

    @pl.when(step == 0)
    def _():
        total_ref[...] = jnp.zeros_like(total_ref)
        for k in range(groups):
            first = (group ^ k) * 2
            at = pl.multiple_of((first + core) * rows, rows)
            amplitudes_ref[pl.ds(at, rows), :] = arrived[k][:rows]
            at = pl.multiple_of((first + 1 - core) * rows, rows)
            amplitudes_ref[pl.ds(at, rows), :] = arrived[k][rows:]

    amplitudes = amplitudes_ref[...]
    for q in range(pairs):
        part = dot(mixed_ref[q, :rows, :], amplitudes)
        line[:, pl.ds(q * columns, columns)] = part.astype(BF16)
    total_ref[...] += dot(line[...], hot_ref[...])

    @pl.when(step == steps - 1)
    def _():
        for k in range(peers):
            part = total_ref[:, pl.ds(pl.multiple_of((column ^ k) * columns, columns), columns)]
            if k == 0:
                own_ref[...] = part
            else:
                sent[k - 1][:rows] = part.astype(BF16)
                sent[k - 1][rows : 2 * rows] = arrived[0][:rows]
                sent[k - 1][2 * rows :] = block_ref[...]


def same_spin_kernel(steps, place, live_ref, code_ref, mixed_ref, one_ref, after_ref, *refs):
    pairs, both, strings = mixed_ref.shape
    side_refs, total_ref = refs[:-1], refs[-1]
    piece, columns = side_refs[0].shape
    half = piece * len(side_refs)
    step = 0 if steps == 1 else pl.program_id(0)
    at = pl.multiple_of(place() * half, half)
    tile = piece
    if steps > 1:

        @pl.when(step == 0)
        def _():
            total_ref[...] = jnp.zeros_like(total_ref)

    for first in range(0, half, tile):
        ids = row_ids(live_ref, at + first, tile, strings)
        total = jnp.zeros((tile, columns), F32) if steps == 1 else total_ref[pl.ds(first, tile), :]
        for q in range(pairs):
            total = total + dot_nt(hot_tile(code_ref[q : q + 1, :], ids), mixed_ref[q, both - columns :, :])
        if steps > 1:
            total_ref[pl.ds(first, tile), :] = total
        one = jnp.transpose(one_ref[both - columns :, pl.ds(at + first, tile)])
        side_refs[first // piece][...] = (one + 0.5 * total).astype(BF16)


def final_kernel(peers, place, alive_ref, own_ref, amplitudes_ref, message_ref, block_ref, *refs):
    out_ref, side_ref = refs[-2:]
    arrived, sides = refs[: peers - 1][::-1], refs[peers - 1 : -2]
    rows, columns = own_ref.shape
    piece = sides[0].shape[0]
    pieces = len(sides) // 2
    core, column = place()
    for i in range(pieces):
        side_ref[pl.ds(pl.multiple_of((core * pieces + i) * piece, piece), piece), :] = sides[i][...]
        at = pl.multiple_of(((1 - core) * pieces + i) * piece, piece)
        side_ref[pl.ds(at, piece), :] = sides[pieces + i][...]
    total = own_ref[...]
    left, right = [], []
    for k in range(peers):
        at = pl.multiple_of((column ^ k) * columns, columns)
        if k == 0:
            left += [block_ref[...], message_ref[:rows]]
        else:
            left += [arrived[k - 1][2 * rows :], arrived[k - 1][rows : 2 * rows]]
            total = total + arrived[k - 1][:rows].astype(F32)
        right += [amplitudes_ref[pl.ds(at, columns), :], side_ref[pl.ds(at, columns), :]]
    total = total + dot(jnp.concatenate(left, 1), jnp.concatenate(right, 0))
    out_ref[...] = (total * alive_ref[...]).astype(BF16)


def per_device(sizes, amplitudes, code, counts, pair_irrep, integrals, one_body):
    rows, columns = amplitudes.shape
    pairs, strings = code.shape
    cap = strings // counts.shape[0]
    groups, peers = sizes[0] // 2, sizes[1]
    both = rows + columns
    resident = pairs * both * strings * 2 <= RESIDENT
    tile = both if resident else 128
    row_tiles = both // tile
    pair_tiles = 1 if resident else pairs // 4
    part = pairs // pair_tiles
    hbm = pl.BlockSpec(memory_space=pl.ANY)
    vmem = pl.BlockSpec(memory_space=pltpu.VMEM)

    def tiled(shape, dim):
        if resident:
            return vmem
        return pl.BlockSpec(shape, lambda i: tuple(i if d == dim else 0 for d in range(len(shape))))

    def shape_of(shape, dtype):
        return pltpu.VMEM(shape, dtype) if resident else jax.ShapeDtypeStruct(shape, dtype)

    def near(value):
        return pltpu.with_memory_space_constraint(value, pltpu.VMEM) if resident else value

    def far(value):
        return pltpu.with_memory_space_constraint(value, pltpu.HBM)

    def call(body, name, tiles, *args, flops=0, **keys):
        if tiles > 1:
            keys["grid"] = (tiles,)
        params = pltpu.CompilerParams(vmem_limit_bytes=NEAR_LIMIT if resident else VMEM_LIMIT)
        cost = pl.CostEstimate(flops=flops, bytes_accessed=0, transcendentals=0)
        return pl.pallas_call(body, name=name, compiler_params=params, cost_estimate=cost, **keys)(*args)

    def alpha():
        return lax.axis_index("aa")

    def beta():
        return lax.axis_index("ba")

    def over_alpha(value, mask):
        return lax.ppermute(value, "aa", [(i, i ^ mask) for i in range(sizes[0])])

    def over_beta(value, mask):
        return lax.ppermute(value, "ba", [(i, i ^ mask) for i in range(peers)])

    def columns_at(code_ref):
        if resident:
            chip = code_ref[:, pl.ds(pl.multiple_of(alpha() // 2 * 2 * rows, 2 * rows), 2 * rows)]
            own = jnp.where(alpha() % 2 == 0, chip[:, :rows], chip[:, rows:])
            return jnp.concatenate([own, code_ref[:, pl.ds(pl.multiple_of(beta() * columns, columns), columns)]], 1)
        at = pl.program_id(0) * tile
        first = jnp.where(at < rows, alpha() * rows + at, beta() * columns + at - rows)
        return code_ref[:, pl.ds(pl.multiple_of(first, tile), tile)]

    sibling = over_alpha(amplitudes, 1)
    codes, live, mixer, alive, own_c = call(
        functools.partial(tables_kernel, cap, lambda: (alpha() * rows, beta() * columns)),
        "tables",
        1,
        far(counts),
        far(pair_irrep),
        far(code),
        far(integrals),
        far(one_body.reshape(1, pairs)),
        far(amplitudes),
        in_specs=[hbm] * 6,
        out_shape=(
            shape_of((pairs, strings), I32),
            shape_of((strings, 128), I32),
            shape_of((pairs * 8 + 8, pairs * 8), BF16),
            shape_of((rows, columns), F32),
            shape_of((rows, columns), BF16),
        ),
        out_specs=(vmem,) * 5,
        scratch_shapes=[
            pltpu.SMEM(counts.shape, I32),
            pltpu.SMEM(pair_irrep.shape, I32),
            pltpu.VMEM((pairs, pairs), BF16),
            pltpu.VMEM((1, pairs), BF16),
            pltpu.SemaphoreType.DMA((6,)),
        ],
    )
    message = call(
        join_kernel,
        "join",
        1,
        near(own_c),
        near(sibling),
        in_specs=[vmem] * 2,
        out_shape=shape_of((2 * rows, columns), BF16),
        out_specs=vmem,
    )
    messages = [message] + [over_alpha(message, 2 * k) for k in range(1, groups)]
    mixed, one = call(
        functools.partial(mix_kernel, columns_at),
        "mix",
        row_tiles,
        near(codes),
        near(live),
        near(mixer),
        near(message),
        flops=2 * both * pairs * pairs * 8 * strings,
        in_specs=[vmem] * 4,
        out_shape=(shape_of((pairs, both, strings), BF16), shape_of((both, strings), F32)),
        out_specs=(tiled((pairs, tile, strings), 1), tiled((tile, strings), 0)),
    )
    code_parts = near(codes) if resident else codes.reshape(pair_tiles, part, strings)
    code_spec = vmem if resident else pl.BlockSpec((None, part, strings), lambda i: (i, 0, 0))
    hot, block = call(
        functools.partial(hot_kernel, pair_tiles, lambda: beta() * columns),
        "hot",
        pair_tiles,
        near(live),
        code_parts,
        near(mixed),
        near(one),
        flops=2 * pairs * rows * columns * strings,
        in_specs=[vmem, code_spec, tiled((part, both, strings), 0), vmem],
        out_shape=(shape_of((pairs * columns, strings), BF16), shape_of((rows, columns), BF16)),
        out_specs=(tiled((part * columns, strings), 0), vmem),
        scratch_shapes=[pltpu.VMEM((columns, rows), F32)],
    )
    outs = call(
        functools.partial(mixed_kernel, pair_tiles, groups, peers, lambda: (alpha() // 2, alpha() % 2, beta())),
        "mixed",
        pair_tiles,
        near(mixed),
        near(hot),
        near(block),
        *[near(m) for m in messages],
        in_specs=[tiled((part, both, strings), 0), tiled((part * columns, strings), 0)] + [vmem] * (groups + 1),
        out_shape=(shape_of((rows, columns), F32), shape_of((strings, columns), BF16))
        + tuple(shape_of((3 * rows, columns), BF16) for _ in range(peers - 1)),
        out_specs=(vmem,) * (peers + 1),
        scratch_shapes=[pltpu.VMEM((rows, part * columns), BF16), pltpu.VMEM((rows, strings), F32)],
    )
    own, gathered = outs[:2]
    arrived = [over_beta(m, k) for k, m in zip(range(peers - 1, 0, -1), outs[2:])]
    pieces = SIDE_PIECES
    sides = call(
        functools.partial(same_spin_kernel, pair_tiles, lambda: alpha() % 2),
        "same_spin",
        pair_tiles,
        near(live),
        code_parts,
        near(mixed),
        near(one),
        near(own),
        flops=2 * columns * pairs * strings * strings,
        in_specs=[vmem, code_spec, tiled((part, both, strings), 0)] + [vmem] * 2,
        out_shape=tuple(shape_of((strings // 2 // pieces, columns), BF16) for _ in range(pieces)),
        out_specs=(vmem,) * pieces,
        scratch_shapes=[pltpu.VMEM((strings // 2, columns), F32)],
    )
    sides = list(sides) + [over_alpha(side, 1) for side in sides]
    return call(
        functools.partial(final_kernel, peers, lambda: (alpha() % 2, beta())),
        "final",
        1,
        near(alive),
        near(own),
        near(gathered),
        near(message),
        near(block),
        *[near(m) for m in arrived],
        *[near(side) for side in sides],
        in_specs=[vmem] * (4 + peers + 2 * pieces),
        out_shape=jax.ShapeDtypeStruct((rows, columns), BF16),
        out_specs=vmem,
        scratch_shapes=[pltpu.VMEM((strings, columns), BF16)],
    )


def solution(mesh):
    placed = (P("aa", "ba"), P(), P(), P(), P(), P())
    sizes = (mesh.shape["aa"], mesh.shape["ba"])
    return jax.shard_map(
        functools.partial(per_device, sizes), mesh=mesh, in_specs=placed, out_specs=P("aa", "ba"), check_vma=False
    )
```

```python
import functools

import jax
import jax.numpy as jnp
from jax import lax
from jax.experimental import pallas as pl
from jax.experimental.pallas import tpu as pltpu
from jax.sharding import PartitionSpec as P

BF16 = jnp.bfloat16
F32 = jnp.float32
I32 = jnp.int32
I16 = jnp.int16
RESIDENT = 8 * 2**20
VMEM_LIMIT = 48 * 2**20
NEAR_LIMIT = 16 * 2**20
SIDE_PIECES = 2


def iota(shape, dim):
    return lax.broadcasted_iota(I32, shape, dim)


def dot(x, y):
    return jnp.dot(x, y, preferred_element_type=F32)


def dot_nt(x, y):
    return lax.dot_general(x, y, (((1,), (1,)), ((), ())), preferred_element_type=F32)


def live_ids(counts_ref, first, shape, dim, cap):
    ids = iota(shape, dim)
    block = ids // cap
    count = jnp.zeros(shape, I32)
    for j in range(shape[dim] // cap):
        count = jnp.where(block == j, counts_ref[first // cap + j], count)
    return jnp.where(ids - block * cap < count, ids + first + 1, -1)


def sign_of(code):
    return jnp.where(code > 0, 1.0, -1.0).astype(F32)


def turned(at, column, columns):
    return ((at // columns) ^ column) * columns + at % columns


def tables_kernel(cap, place, counts_hbm, irrep_hbm, code_hbm, integrals_hbm, gains_hbm, amplitudes_hbm, *refs):
    code_ref, live_ref, lane_ref, mixer_ref, alive_ref, amplitudes_ref = refs[:6]
    counts_ref, irrep_ref, integrals_ref, gains_ref, plain_ref, sems = refs[6:]
    pairs, strings = code_ref.shape
    rows, columns = amplitudes_ref.shape
    first_a, column = place()
    first_b = column * columns
    copies = [
        pltpu.make_async_copy(source, target, sems.at[i])
        for i, (source, target) in enumerate(
            (
                (irrep_hbm, irrep_ref),
                (integrals_hbm, integrals_ref),
                (gains_hbm, gains_ref),
                (counts_hbm, counts_ref),
                (code_hbm, plain_ref),
                (amplitudes_hbm, amplitudes_ref),
            )
        )
    ]
    for copy in copies:
        copy.start()
    wide = pairs * 8
    spread_q = jnp.where(iota((wide, pairs), 0) // 8 == iota((wide, pairs), 1), 1.0, 0.0).astype(BF16)
    spread_p = jnp.where(iota((pairs, wide), 1) % pairs == iota((pairs, wide), 0), 1.0, 0.0).astype(BF16)
    for copy in copies:
        copy.wait()
    irrep_p = jnp.zeros((pairs, pairs), I32)
    irrep_q = jnp.zeros((pairs, pairs), I32)
    for p in range(pairs):
        irrep_p = jnp.where(iota((pairs, pairs), 0) == p, irrep_ref[p], irrep_p)
        irrep_q = jnp.where(iota((pairs, pairs), 1) == p, irrep_ref[p], irrep_q)
    weights = jnp.where(irrep_p == irrep_q, integrals_ref[...].astype(F32), 0.0).astype(BF16)
    left = jnp.concatenate(
        [dot_nt(spread_q, weights), jnp.broadcast_to(gains_ref[...].astype(F32), (8, pairs))], 0
    ).astype(BF16)
    mixer = dot(left, spread_p)
    same = iota(mixer.shape, 0) % 8 == iota(mixer.shape, 1) // pairs
    mixer_ref[...] = jnp.where(same, mixer, 0.0).astype(BF16)
    within = iota((cap, 128), 0)
    for block in range(strings // cap):
        at = block * cap
        live_ref[pl.ds(at, cap), :] = jnp.where(within < counts_ref[block], within + (at + 1), -1)
    for k in range(strings // columns):
        at = pl.multiple_of((column ^ k) * columns, columns)
        code_ref[:, k * columns : (k + 1) * columns] = plain_ref[:, pl.ds(at, columns)]
        lane_ref[:, k * columns : (k + 1) * columns] = live_ids(counts_ref, at, (8, columns), 1, cap)
    live_a = live_ids(counts_ref, first_a, (rows, columns), 0, cap)
    live_b = live_ids(counts_ref, first_b, (1, columns), 1, cap)
    alive_ref[...] = jnp.where((live_a > 0) & (live_b > 0), 1.0, 0.0)


def join_kernel(own_ref, sibling_ref, message_ref):
    rows = own_ref.shape[0]
    message_ref[:rows] = own_ref[...]
    message_ref[rows:] = sibling_ref[...]


def mix_kernel(columns_at, code_ref, lane_ref, mixer_ref, after_ref, mixed_ref, one_ref):
    pairs, strings = code_ref.shape
    wide = pairs * 8
    ids = jnp.broadcast_to(lane_ref[:1, :], (pairs, strings)).astype(I16)
    zero = jnp.zeros(ids.shape, BF16)
    mixer = mixer_ref[...]
    code = columns_at(code_ref)
    size = jnp.abs(code)
    sign = sign_of(code)

    def along(table, at, dtype):
        tile = jnp.broadcast_to(table[:, at : at + 1], (pairs, 128)).astype(dtype)
        return jnp.concatenate([tile] * (strings // 128), 1)

    for base in range(0, code.shape[1], 16):
        halves = []
        for low in (base, base + 8):
            hot = jnp.concatenate(
                [
                    jnp.where(along(size, a, I16) == ids, along(sign, a, BF16), zero)
                    for a in range(low, low + 8)
                ],
                0,
            )
            part = dot(mixer, hot)
            one_ref[pl.ds(low, 8), :] = part[wide:]
            halves.append(part[:wide].reshape(pairs, 8, strings))
        mixed_ref[:, pl.ds(base, 16), :] = jnp.concatenate(halves, 1).astype(BF16)


def hot_tile(code, ids):
    rows, strings = ids.shape
    size = jnp.broadcast_to(jnp.abs(code), (16, strings)).astype(I16)
    sign = jnp.broadcast_to(sign_of(code), (16, strings)).astype(BF16)
    size = jnp.concatenate([size] * (rows // 16), 0)
    sign = jnp.concatenate([sign] * (rows // 16), 0)
    return jnp.where(size == ids, sign, jnp.zeros(ids.shape, BF16))


def row_ids(live_ref, first, rows, strings):
    return jnp.concatenate([live_ref[pl.ds(first, rows), :]] * (strings // 128), 1).astype(I16)


def hot_kernel(steps, place, live_ref, code_ref, mixed_ref, one_ref, hot_ref, block_ref, total_ref):
    pairs, strings = code_ref.shape
    rows, columns = block_ref.shape
    step = 0 if steps == 1 else pl.program_id(0)
    column = place()
    first = pl.multiple_of(column * columns, columns)
    ids = row_ids(live_ref, first, columns, strings)
    if steps > 1:

        @pl.when(step == 0)
        def _():
            total_ref[...] = jnp.zeros_like(total_ref)

    total = jnp.zeros((columns, rows), F32) if steps == 1 else total_ref[...]
    for q in range(pairs):
        hot = hot_tile(code_ref[q : q + 1, :], ids)
        hot_ref[pl.ds(q * columns, columns), :] = hot
        total = total + dot_nt(hot, mixed_ref[q, :rows, :])
    if steps > 1:
        total_ref[...] = total
    block_ref[...] = (one_ref[:rows, :columns] + 0.5 * jnp.transpose(total)).astype(BF16)


def mixed_kernel(steps, groups, peers, place, mixed_ref, hot_ref, block_ref, *refs):
    arrived = refs[:groups]
    own_ref, amplitudes_ref = refs[groups : groups + 2]
    sent = refs[groups + 2 : groups + 1 + peers][::-1]
    line, total_ref = refs[groups + 1 + peers :]
    pairs, strings = mixed_ref.shape[0], mixed_ref.shape[2]
    rows, columns = block_ref.shape
    step = 0 if steps == 1 else pl.program_id(0)
    group, core, column = place()

    @pl.when(step == 0)
    def _():
        if steps > 1:
            total_ref[...] = jnp.zeros_like(total_ref)
        for k in range(groups):
            first = (group ^ k) * 2
            at = pl.multiple_of(turned((first + core) * rows, column, columns), rows)
            amplitudes_ref[pl.ds(at, rows), :] = arrived[k][:rows]
            at = pl.multiple_of(turned((first + 1 - core) * rows, column, columns), rows)
            amplitudes_ref[pl.ds(at, rows), :] = arrived[k][rows:]

    if steps == 1:
        line = own_ref
    amplitudes = amplitudes_ref[...]
    for q in range(pairs):
        part = dot(mixed_ref[q, :rows, :], amplitudes)
        line[:, pl.ds(q * columns, columns)] = part.astype(BF16)
    if steps == 1:
        total = dot(line[...], hot_ref[:, columns:])
    else:
        total_ref[...] += dot(line[...], hot_ref[...])

    @pl.when(step == steps - 1)
    def _():
        if steps > 1:
            own_ref[...] = total_ref[:, :columns]
        for k in range(1, peers):
            if steps == 1:
                part = total[:, (k - 1) * columns : k * columns]
            else:
                part = total_ref[:, pl.ds(k * columns, columns)]
            sent[k - 1][:rows] = part.astype(BF16)
            sent[k - 1][rows : 2 * rows] = arrived[0][:rows]
            sent[k - 1][2 * rows :] = block_ref[...]


def same_spin_kernel(steps, place, live_ref, code_ref, mixed_ref, one_ref, part_ref, hot_ref, *refs):
    pairs, both, strings = mixed_ref.shape
    own_ref, side_refs, total_ref = refs[0], refs[1:-1], refs[-1]
    piece, columns = side_refs[0].shape
    half = piece * len(side_refs)
    step = 0 if steps == 1 else pl.program_id(0)
    core, column = place()
    at = pl.multiple_of(core * half, half)
    width = min(piece, columns)
    tile = piece
    if steps == 1:
        own_ref[...] = dot(part_ref[...], hot_ref[:, :columns])
    else:
        own_ref[...] = part_ref[...]
    if steps > 1:

        @pl.when(step == 0)
        def _():
            total_ref[...] = jnp.zeros_like(total_ref)

    for first in range(0, half, tile):
        ids = row_ids(live_ref, at + first, tile, strings)
        total = jnp.zeros((tile, columns), F32) if steps == 1 else total_ref[pl.ds(first, tile), :]
        for q in range(pairs):
            total = total + dot_nt(hot_tile(code_ref[q : q + 1, :], ids), mixed_ref[q, both - columns :, :])
        if steps > 1:
            total_ref[pl.ds(first, tile), :] = total
        blocks = [
            one_ref[both - columns :, pl.ds(pl.multiple_of(turned(at + low, column, columns), width), width)]
            for low in range(first, first + tile, width)
        ]
        one = jnp.transpose(jnp.concatenate(blocks, 1))
        side_refs[first // piece][...] = (one + 0.5 * total).astype(BF16)


def final_kernel(peers, place, alive_ref, own_ref, amplitudes_ref, message_ref, block_ref, *refs):
    out_ref, side_ref = refs[-2:]
    arrived, sides = refs[: peers - 1][::-1], refs[peers - 1 : -2]
    rows, columns = own_ref.shape
    piece = sides[0].shape[0]
    pieces = len(sides) // 2
    core, column = place()
    for i in range(pieces):
        side_ref[pl.ds(pl.multiple_of((core * pieces + i) * piece, piece), piece), :] = sides[i][...]
        at = pl.multiple_of(((1 - core) * pieces + i) * piece, piece)
        side_ref[pl.ds(at, piece), :] = sides[pieces + i][...]
    total = own_ref[...]
    left, right = [], []
    for k in range(peers):
        at = pl.multiple_of((column ^ k) * columns, columns)
        if k == 0:
            left += [block_ref[...], message_ref[:rows]]
        else:
            left += [arrived[k - 1][2 * rows :], arrived[k - 1][rows : 2 * rows]]
            total = total + arrived[k - 1][:rows].astype(F32)
        right += [amplitudes_ref[k * columns : (k + 1) * columns, :], side_ref[pl.ds(at, columns), :]]
    total = total + dot(jnp.concatenate(left, 1), jnp.concatenate(right, 0))
    out_ref[...] = (total * alive_ref[...]).astype(BF16)


def per_device(sizes, amplitudes, code, counts, pair_irrep, integrals, one_body):
    rows, columns = amplitudes.shape
    pairs, strings = code.shape
    cap = strings // counts.shape[0]
    groups, peers = sizes[0] // 2, sizes[1]
    both = rows + columns
    resident = pairs * both * strings * 2 <= RESIDENT
    tile = both if resident else 128
    row_tiles = both // tile
    pair_tiles = 1 if resident else pairs // 4
    part = pairs // pair_tiles
    hbm = pl.BlockSpec(memory_space=pl.ANY)
    vmem = pl.BlockSpec(memory_space=pltpu.VMEM)

    def tiled(shape, dim):
        if resident:
            return vmem
        return pl.BlockSpec(shape, lambda i: tuple(i if d == dim else 0 for d in range(len(shape))))

    def shape_of(shape, dtype):
        return pltpu.VMEM(shape, dtype) if resident else jax.ShapeDtypeStruct(shape, dtype)

    def near(value):
        return pltpu.with_memory_space_constraint(value, pltpu.VMEM) if resident else value

    def far(value):
        return pltpu.with_memory_space_constraint(value, pltpu.HBM)

    def call(body, name, tiles, *args, flops=0, **keys):
        if tiles > 1:
            keys["grid"] = (tiles,)
        params = pltpu.CompilerParams(vmem_limit_bytes=NEAR_LIMIT if resident else VMEM_LIMIT)
        cost = pl.CostEstimate(flops=flops, bytes_accessed=0, transcendentals=0)
        return pl.pallas_call(body, name=name, compiler_params=params, cost_estimate=cost, **keys)(*args)

    def alpha():
        return lax.axis_index("aa")

    def beta():
        return lax.axis_index("ba")

    def over_alpha(value, mask):
        return lax.ppermute(value, "aa", [(i, i ^ mask) for i in range(sizes[0])])

    def over_beta(value, mask):
        return lax.ppermute(value, "ba", [(i, i ^ mask) for i in range(peers)])

    def columns_at(code_ref):
        if resident:
            at = turned(alpha() // 2 * 2 * rows, beta(), columns)
            chip = code_ref[:, pl.ds(pl.multiple_of(at, 2 * rows), 2 * rows)]
            own = jnp.where(alpha() % 2 == 0, chip[:, :rows], chip[:, rows:])
            return jnp.concatenate([own, code_ref[:, :columns]], 1)
        at = pl.program_id(0) * tile
        first = jnp.where(at < rows, alpha() * rows + at, beta() * columns + at - rows)
        return code_ref[:, pl.ds(pl.multiple_of(turned(first, beta(), columns), tile), tile)]

    sibling = over_alpha(amplitudes, 1)
    codes, live, lane, mixer, alive, own_c = call(
        functools.partial(tables_kernel, cap, lambda: (alpha() * rows, beta())),
        "tables",
        1,
        far(counts),
        far(pair_irrep),
        far(code),
        far(integrals),
        far(one_body.reshape(1, pairs)),
        far(amplitudes),
        in_specs=[hbm] * 6,
        out_shape=(
            shape_of((pairs, strings), I32),
            shape_of((strings, 128), I32),
            shape_of((8, strings), I32),
            shape_of((pairs * 8 + 8, pairs * 8), BF16),
            shape_of((rows, columns), F32),
            shape_of((rows, columns), BF16),
        ),
        out_specs=(vmem,) * 6,
        scratch_shapes=[
            pltpu.SMEM(counts.shape, I32),
            pltpu.SMEM(pair_irrep.shape, I32),
            pltpu.VMEM((pairs, pairs), BF16),
            pltpu.VMEM((1, pairs), BF16),
            pltpu.VMEM((pairs, strings), I32),
            pltpu.SemaphoreType.DMA((6,)),
        ],
    )
    message = call(
        join_kernel,
        "join",
        1,
        near(own_c),
        near(sibling),
        in_specs=[vmem] * 2,
        out_shape=shape_of((2 * rows, columns), BF16),
        out_specs=vmem,
    )
    messages = [message] + [over_alpha(message, 2 * k) for k in range(1, groups)]
    mixed, one = call(
        functools.partial(mix_kernel, columns_at),
        "mix",
        row_tiles,
        near(codes),
        near(lane),
        near(mixer),
        near(message),
        flops=2 * both * pairs * pairs * 8 * strings,
        in_specs=[vmem] * 4,
        out_shape=(shape_of((pairs, both, strings), BF16), shape_of((both, strings), F32)),
        out_specs=(tiled((pairs, tile, strings), 1), tiled((tile, strings), 0)),
    )
    code_parts = near(codes) if resident else codes.reshape(pair_tiles, part, strings)
    code_spec = vmem if resident else pl.BlockSpec((None, part, strings), lambda i: (i, 0, 0))
    hot, block = call(
        functools.partial(hot_kernel, pair_tiles, beta),
        "hot",
        pair_tiles,
        near(live),
        code_parts,
        near(mixed),
        near(one),
        flops=2 * pairs * rows * columns * strings,
        in_specs=[vmem, code_spec, tiled((part, both, strings), 0), vmem],
        out_shape=(shape_of((pairs * columns, strings), BF16), shape_of((rows, columns), BF16)),
        out_specs=(tiled((part * columns, strings), 0), vmem),
        scratch_shapes=[pltpu.VMEM((columns, rows), F32)],
    )
    outs = call(
        functools.partial(mixed_kernel, pair_tiles, groups, peers, lambda: (alpha() // 2, alpha() % 2, beta())),
        "mixed",
        pair_tiles,
        near(mixed),
        near(hot),
        near(block),
        *[near(m) for m in messages],
        in_specs=[tiled((part, both, strings), 0), tiled((part * columns, strings), 0)] + [vmem] * (groups + 1),
        out_shape=(
            shape_of((rows, pairs * columns), BF16) if resident else shape_of((rows, columns), F32),
            shape_of((strings, columns), BF16),
        )
        + tuple(shape_of((3 * rows, columns), BF16) for _ in range(peers - 1)),
        out_specs=(vmem,) * (peers + 1),
        scratch_shapes=[pltpu.VMEM((rows, part * columns), BF16), pltpu.VMEM((rows, strings), F32)],
    )
    own, gathered = outs[:2]
    arrived = [over_beta(m, k) for k, m in zip(range(peers - 1, 0, -1), outs[2:])]
    pieces = SIDE_PIECES
    own, *sides = call(
        functools.partial(same_spin_kernel, pair_tiles, lambda: (alpha() % 2, beta())),
        "same_spin",
        pair_tiles,
        near(live),
        code_parts,
        near(mixed),
        near(one),
        near(own),
        near(hot) if resident else hot[:16, :128],
        flops=2 * columns * pairs * strings * strings,
        in_specs=[vmem, code_spec, tiled((part, both, strings), 0)] + [vmem] * 3,
        out_shape=(shape_of((rows, columns), F32),)
        + tuple(shape_of((strings // 2 // pieces, columns), BF16) for _ in range(pieces)),
        out_specs=(vmem,) * (1 + pieces),
        scratch_shapes=[pltpu.VMEM((strings // 2, columns), F32)],
    )
    sides = list(sides) + [over_alpha(side, 1) for side in sides]
    return call(
        functools.partial(final_kernel, peers, lambda: (alpha() % 2, beta())),
        "final",
        1,
        near(alive),
        near(own),
        near(gathered),
        near(message),
        near(block),
        *[near(m) for m in arrived],
        *[near(side) for side in sides],
        in_specs=[vmem] * (4 + peers + 2 * pieces),
        out_shape=jax.ShapeDtypeStruct((rows, columns), BF16),
        out_specs=vmem,
        scratch_shapes=[pltpu.VMEM((strings, columns), BF16)],
    )


def solution(mesh):
    placed = (P("aa", "ba"), P(), P(), P(), P(), P())
    sizes = (mesh.shape["aa"], mesh.shape["ba"])
    return jax.shard_map(
        functools.partial(per_device, sizes), mesh=mesh, in_specs=placed, out_specs=P("aa", "ba"), check_vma=False
    )
```

```python
import functools

import jax
import jax.numpy as jnp
from jax import lax
from jax.experimental import pallas as pl
from jax.experimental.pallas import tpu as pltpu
from jax.sharding import PartitionSpec as P

BF16 = jnp.bfloat16
F32 = jnp.float32
I32 = jnp.int32
I16 = jnp.int16
RESIDENT = 8 * 2**20
VMEM_LIMIT = 48 * 2**20
NEAR_LIMIT = 16 * 2**20
SIDE_PIECES = 2


def iota(shape, dim):
    return lax.broadcasted_iota(I32, shape, dim)


def dot(x, y):
    return jnp.dot(x, y, preferred_element_type=F32)


def dot_nt(x, y):
    return lax.dot_general(x, y, (((1,), (1,)), ((), ())), preferred_element_type=F32)


def live_ids(counts_ref, first, shape, dim, cap):
    ids = iota(shape, dim)
    block = ids // cap
    count = jnp.zeros(shape, I32)
    for j in range(shape[dim] // cap):
        count = jnp.where(block == j, counts_ref[first // cap + j], count)
    return jnp.where(ids - block * cap < count, ids + first + 1, -1)


def sign_of(code):
    return jnp.where(code > 0, 1.0, -1.0).astype(F32)


def by_start(peers):
    return (*range(2, peers), 1)


def turned(at, column, columns):
    return ((at // columns) ^ column) * columns + at % columns


def tables_kernel(cap, place, counts_hbm, irrep_hbm, code_hbm, integrals_hbm, gains_hbm, amplitudes_hbm, *refs):
    code_ref, live_ref, lane_ref, mixer_ref, alive_ref, amplitudes_ref = refs[:6]
    counts_ref, irrep_ref, integrals_ref, gains_ref, plain_ref, sems = refs[6:]
    pairs, strings = code_ref.shape
    rows, columns = amplitudes_ref.shape
    first_a, column = place()
    first_b = column * columns
    copies = [
        pltpu.make_async_copy(source, target, sems.at[i])
        for i, (source, target) in enumerate(
            (
                (irrep_hbm, irrep_ref),
                (integrals_hbm, integrals_ref),
                (gains_hbm, gains_ref),
                (counts_hbm, counts_ref),
                (code_hbm, plain_ref),
                (amplitudes_hbm, amplitudes_ref),
            )
        )
    ]
    for copy in copies:
        copy.start()
    wide = pairs * 8
    spread_q = jnp.where(iota((wide, pairs), 0) // 8 == iota((wide, pairs), 1), 1.0, 0.0).astype(BF16)
    spread_p = jnp.where(iota((pairs, wide), 1) % pairs == iota((pairs, wide), 0), 1.0, 0.0).astype(BF16)
    for copy in copies:
        copy.wait()
    irrep_p = jnp.zeros((pairs, pairs), I32)
    irrep_q = jnp.zeros((pairs, pairs), I32)
    for p in range(pairs):
        irrep_p = jnp.where(iota((pairs, pairs), 0) == p, irrep_ref[p], irrep_p)
        irrep_q = jnp.where(iota((pairs, pairs), 1) == p, irrep_ref[p], irrep_q)
    weights = jnp.where(irrep_p == irrep_q, integrals_ref[...].astype(F32), 0.0).astype(BF16)
    left = jnp.concatenate(
        [dot_nt(spread_q, weights), jnp.broadcast_to(gains_ref[...].astype(F32), (8, pairs))], 0
    ).astype(BF16)
    mixer = dot(left, spread_p)
    same = iota(mixer.shape, 0) % 8 == iota(mixer.shape, 1) // pairs
    mixer_ref[...] = jnp.where(same, mixer, 0.0).astype(BF16)
    within = iota((cap, 128), 0)
    for block in range(strings // cap):
        at = block * cap
        live_ref[pl.ds(at, cap), :] = jnp.where(within < counts_ref[block], within + (at + 1), -1)
    for k in range(strings // columns):
        at = pl.multiple_of((column ^ k) * columns, columns)
        code_ref[:, k * columns : (k + 1) * columns] = plain_ref[:, pl.ds(at, columns)]
        lane_ref[:, k * columns : (k + 1) * columns] = live_ids(counts_ref, at, (8, columns), 1, cap)
    live_a = live_ids(counts_ref, first_a, (rows, columns), 0, cap)
    live_b = live_ids(counts_ref, first_b, (1, columns), 1, cap)
    alive_ref[...] = jnp.where((live_a > 0) & (live_b > 0), 1.0, 0.0)


def join_kernel(own_ref, sibling_ref, message_ref):
    rows = own_ref.shape[0]
    message_ref[:rows] = own_ref[...]
    message_ref[rows:] = sibling_ref[...]


def mix_kernel(columns_at, code_ref, lane_ref, mixer_ref, after_ref, mixed_ref, one_ref):
    pairs, strings = code_ref.shape
    wide = pairs * 8
    ids = jnp.broadcast_to(lane_ref[:1, :], (pairs, strings)).astype(I16)
    zero = jnp.zeros(ids.shape, BF16)
    mixer = mixer_ref[...]
    code = columns_at(code_ref)
    size = jnp.abs(code)
    sign = sign_of(code)

    def along(table, at, dtype):
        tile = jnp.broadcast_to(table[:, at : at + 1], (pairs, 128)).astype(dtype)
        return jnp.concatenate([tile] * (strings // 128), 1)

    for base in range(0, code.shape[1], 16):
        halves = []
        for low in (base, base + 8):
            hot = jnp.concatenate(
                [
                    jnp.where(along(size, a, I16) == ids, along(sign, a, BF16), zero)
                    for a in range(low, low + 8)
                ],
                0,
            )
            part = dot(mixer, hot)
            one_ref[pl.ds(low, 8), :] = part[wide:]
            halves.append(part[:wide].reshape(pairs, 8, strings))
        mixed_ref[:, pl.ds(base, 16), :] = jnp.concatenate(halves, 1).astype(BF16)


def hot_tile(code, ids):
    rows, strings = ids.shape
    size = jnp.broadcast_to(jnp.abs(code), (16, strings)).astype(I16)
    sign = jnp.broadcast_to(sign_of(code), (16, strings)).astype(BF16)
    size = jnp.concatenate([size] * (rows // 16), 0)
    sign = jnp.concatenate([sign] * (rows // 16), 0)
    return jnp.where(size == ids, sign, jnp.zeros(ids.shape, BF16))


def row_ids(live_ref, first, rows, strings):
    return jnp.concatenate([live_ref[pl.ds(first, rows), :]] * (strings // 128), 1).astype(I16)


def hot_kernel(steps, place, live_ref, code_ref, mixed_ref, one_ref, hot_ref, block_ref, total_ref):
    pairs, strings = code_ref.shape
    rows, columns = block_ref.shape
    step = 0 if steps == 1 else pl.program_id(0)
    column = place()
    first = pl.multiple_of(column * columns, columns)
    ids = row_ids(live_ref, first, columns, strings)
    if steps > 1:

        @pl.when(step == 0)
        def _():
            total_ref[...] = jnp.zeros_like(total_ref)

    total = jnp.zeros((columns, rows), F32) if steps == 1 else total_ref[...]
    for q in range(pairs):
        hot = hot_tile(code_ref[q : q + 1, :], ids)
        hot_ref[pl.ds(q * columns, columns), :] = hot
        total = total + dot_nt(hot, mixed_ref[q, :rows, :])
    if steps > 1:
        total_ref[...] = total
    block_ref[...] = (one_ref[:rows, :columns] + 0.5 * jnp.transpose(total)).astype(BF16)


def mixed_kernel(steps, groups, peers, place, mixed_ref, hot_ref, block_ref, *refs):
    arrived = refs[:groups]
    own_ref, amplitudes_ref = refs[groups : groups + 2]
    sent = [refs[groups + 2 + by_start(peers).index(k)] for k in range(1, peers)]
    line, total_ref = refs[groups + 1 + peers :]
    pairs, strings = mixed_ref.shape[0], mixed_ref.shape[2]
    rows, columns = block_ref.shape
    step = 0 if steps == 1 else pl.program_id(0)
    group, core, column = place()

    @pl.when(step == 0)
    def _():
        if steps > 1:
            total_ref[...] = jnp.zeros_like(total_ref)
        for k in range(groups):
            first = (group ^ k) * 2
            at = pl.multiple_of(turned((first + core) * rows, column, columns), rows)
            amplitudes_ref[pl.ds(at, rows), :] = arrived[k][:rows]
            at = pl.multiple_of(turned((first + 1 - core) * rows, column, columns), rows)
            amplitudes_ref[pl.ds(at, rows), :] = arrived[k][rows:]

    if steps == 1:
        line = own_ref
    amplitudes = amplitudes_ref[...]
    for low in range(0, pairs, 4):
        part = dot(mixed_ref[low : low + 4, :rows, :].reshape(4 * rows, strings), amplitudes).astype(BF16)
        for q in range(4):
            line[:, pl.ds((low + q) * columns, columns)] = part[q * rows : (q + 1) * rows]
    if steps == 1:
        total = dot(line[...], hot_ref[:, columns:])
    else:
        total_ref[...] += dot(line[...], hot_ref[...])

    @pl.when(step == steps - 1)
    def _():
        if steps > 1:
            own_ref[...] = total_ref[:, :columns]
        for k in range(1, peers):
            if steps == 1:
                part = total[:, (k - 1) * columns : k * columns]
            else:
                part = total_ref[:, pl.ds(k * columns, columns)]
            sent[k - 1][:rows] = part.astype(BF16)
            sent[k - 1][rows : 2 * rows] = arrived[0][:rows]
            sent[k - 1][2 * rows :] = block_ref[...]


def same_spin_kernel(steps, place, live_ref, code_ref, mixed_ref, one_ref, part_ref, hot_ref, *refs):
    pairs, both, strings = mixed_ref.shape
    own_ref, side_refs, total_ref = refs[0], refs[1:-1], refs[-1]
    piece, columns = side_refs[0].shape
    half = piece * len(side_refs)
    step = 0 if steps == 1 else pl.program_id(0)
    core, column = place()
    at = pl.multiple_of(core * half, half)
    width = min(piece, columns)
    tile = piece
    if steps == 1:
        own_ref[...] = dot(part_ref[...], hot_ref[:, :columns])
    else:
        own_ref[...] = part_ref[...]
    if steps > 1:

        @pl.when(step == 0)
        def _():
            total_ref[...] = jnp.zeros_like(total_ref)

    for first in range(0, half, tile):
        ids = row_ids(live_ref, at + first, tile, strings)
        total = jnp.zeros((tile, columns), F32) if steps == 1 else total_ref[pl.ds(first, tile), :]
        for q in range(pairs):
            total = total + dot_nt(hot_tile(code_ref[q : q + 1, :], ids), mixed_ref[q, both - columns :, :])
        if steps > 1:
            total_ref[pl.ds(first, tile), :] = total
        blocks = [
            one_ref[both - columns :, pl.ds(pl.multiple_of(turned(at + low, column, columns), width), width)]
            for low in range(first, first + tile, width)
        ]
        one = jnp.transpose(jnp.concatenate(blocks, 1))
        side_refs[first // piece][...] = (one + 0.5 * total).astype(BF16)


def final_kernel(peers, place, alive_ref, own_ref, amplitudes_ref, message_ref, block_ref, *refs):
    out_ref, side_ref = refs[-2:]
    arrived, sides = [refs[by_start(peers).index(k)] for k in range(1, peers)], refs[peers - 1 : -2]
    rows, columns = own_ref.shape
    piece = sides[0].shape[0]
    pieces = len(sides) // 2
    core, column = place()
    for i in range(pieces):
        side_ref[pl.ds(pl.multiple_of((core * pieces + i) * piece, piece), piece), :] = sides[i][...]
        at = pl.multiple_of(((1 - core) * pieces + i) * piece, piece)
        side_ref[pl.ds(at, piece), :] = sides[pieces + i][...]
    total = own_ref[...]
    left, right = [], []
    for k in range(peers):
        at = pl.multiple_of((column ^ k) * columns, columns)
        if k == 0:
            left += [block_ref[...], message_ref[:rows]]
        else:
            left += [arrived[k - 1][2 * rows :], arrived[k - 1][rows : 2 * rows]]
            total = total + arrived[k - 1][:rows].astype(F32)
        right += [amplitudes_ref[k * columns : (k + 1) * columns, :], side_ref[pl.ds(at, columns), :]]
    total = total + dot(jnp.concatenate(left, 1), jnp.concatenate(right, 0))
    out_ref[...] = (total * alive_ref[...]).astype(BF16)


def per_device(sizes, amplitudes, code, counts, pair_irrep, integrals, one_body):
    rows, columns = amplitudes.shape
    pairs, strings = code.shape
    cap = strings // counts.shape[0]
    groups, peers = sizes[0] // 2, sizes[1]
    both = rows + columns
    resident = pairs * both * strings * 2 <= RESIDENT
    tile = both if resident else 128
    row_tiles = both // tile
    pair_tiles = 1 if resident else pairs // 4
    part = pairs // pair_tiles
    hbm = pl.BlockSpec(memory_space=pl.ANY)
    vmem = pl.BlockSpec(memory_space=pltpu.VMEM)

    def tiled(shape, dim):
        if resident:
            return vmem
        return pl.BlockSpec(shape, lambda i: tuple(i if d == dim else 0 for d in range(len(shape))))

    def shape_of(shape, dtype):
        return pltpu.VMEM(shape, dtype) if resident else jax.ShapeDtypeStruct(shape, dtype)

    def near(value):
        return pltpu.with_memory_space_constraint(value, pltpu.VMEM) if resident else value

    def far(value):
        return pltpu.with_memory_space_constraint(value, pltpu.HBM)

    def call(body, name, tiles, *args, flops=0, **keys):
        if tiles > 1:
            keys["grid"] = (tiles,)
        params = pltpu.CompilerParams(vmem_limit_bytes=NEAR_LIMIT if resident else VMEM_LIMIT)
        cost = pl.CostEstimate(flops=flops, bytes_accessed=0, transcendentals=0)
        return pl.pallas_call(body, name=name, compiler_params=params, cost_estimate=cost, **keys)(*args)

    def alpha():
        return lax.axis_index("aa")

    def beta():
        return lax.axis_index("ba")

    def over_alpha(value, mask):
        return lax.ppermute(value, "aa", [(i, i ^ mask) for i in range(sizes[0])])

    def over_beta(value, mask):
        return lax.ppermute(value, "ba", [(i, i ^ mask) for i in range(peers)])

    def columns_at(code_ref):
        if resident:
            at = turned(alpha() // 2 * 2 * rows, beta(), columns)
            chip = code_ref[:, pl.ds(pl.multiple_of(at, 2 * rows), 2 * rows)]
            own = jnp.where(alpha() % 2 == 0, chip[:, :rows], chip[:, rows:])
            return jnp.concatenate([own, code_ref[:, :columns]], 1)
        at = pl.program_id(0) * tile
        first = jnp.where(at < rows, alpha() * rows + at, beta() * columns + at - rows)
        return code_ref[:, pl.ds(pl.multiple_of(turned(first, beta(), columns), tile), tile)]

    sibling = over_alpha(amplitudes, 1)
    codes, live, lane, mixer, alive, own_c = call(
        functools.partial(tables_kernel, cap, lambda: (alpha() * rows, beta())),
        "tables",
        1,
        far(counts),
        far(pair_irrep),
        far(code),
        far(integrals),
        far(one_body.reshape(1, pairs)),
        far(amplitudes),
        in_specs=[hbm] * 6,
        out_shape=(
            shape_of((pairs, strings), I32),
            shape_of((strings, 128), I32),
            shape_of((8, strings), I32),
            shape_of((pairs * 8 + 8, pairs * 8), BF16),
            shape_of((rows, columns), F32),
            shape_of((rows, columns), BF16),
        ),
        out_specs=(vmem,) * 6,
        scratch_shapes=[
            pltpu.SMEM(counts.shape, I32),
            pltpu.SMEM(pair_irrep.shape, I32),
            pltpu.VMEM((pairs, pairs), BF16),
            pltpu.VMEM((1, pairs), BF16),
            pltpu.VMEM((pairs, strings), I32),
            pltpu.SemaphoreType.DMA((6,)),
        ],
    )
    message = call(
        join_kernel,
        "join",
        1,
        near(own_c),
        near(sibling),
        in_specs=[vmem] * 2,
        out_shape=shape_of((2 * rows, columns), BF16),
        out_specs=vmem,
    )
    messages = [message] + [over_alpha(message, 2 * k) for k in range(1, groups)]
    mixed, one = call(
        functools.partial(mix_kernel, columns_at),
        "mix",
        row_tiles,
        near(codes),
        near(lane),
        near(mixer),
        near(message),
        flops=2 * both * pairs * pairs * 8 * strings,
        in_specs=[vmem] * 4,
        out_shape=(shape_of((pairs, both, strings), BF16), shape_of((both, strings), F32)),
        out_specs=(tiled((pairs, tile, strings), 1), tiled((tile, strings), 0)),
    )
    code_parts = near(codes) if resident else codes.reshape(pair_tiles, part, strings)
    code_spec = vmem if resident else pl.BlockSpec((None, part, strings), lambda i: (i, 0, 0))
    hot, block = call(
        functools.partial(hot_kernel, pair_tiles, beta),
        "hot",
        pair_tiles,
        near(live),
        code_parts,
        near(mixed),
        near(one),
        flops=2 * pairs * rows * columns * strings,
        in_specs=[vmem, code_spec, tiled((part, both, strings), 0), vmem],
        out_shape=(shape_of((pairs * columns, strings), BF16), shape_of((rows, columns), BF16)),
        out_specs=(tiled((part * columns, strings), 0), vmem),
        scratch_shapes=[pltpu.VMEM((columns, rows), F32)],
    )
    outs = call(
        functools.partial(mixed_kernel, pair_tiles, groups, peers, lambda: (alpha() // 2, alpha() % 2, beta())),
        "mixed",
        pair_tiles,
        near(mixed),
        near(hot),
        near(block),
        *[near(m) for m in messages],
        in_specs=[tiled((part, both, strings), 0), tiled((part * columns, strings), 0)] + [vmem] * (groups + 1),
        out_shape=(
            shape_of((rows, pairs * columns), BF16) if resident else shape_of((rows, columns), F32),
            shape_of((strings, columns), BF16),
        )
        + tuple(shape_of((3 * rows, columns), BF16) for _ in range(peers - 1)),
        out_specs=(vmem,) * (peers + 1),
        scratch_shapes=[pltpu.VMEM((rows, part * columns), BF16), pltpu.VMEM((rows, strings), F32)],
    )
    own, gathered = outs[:2]
    arrived = [over_beta(m, k) for k, m in zip(by_start(peers), outs[2:])]
    pieces = SIDE_PIECES
    own, *sides = call(
        functools.partial(same_spin_kernel, pair_tiles, lambda: (alpha() % 2, beta())),
        "same_spin",
        pair_tiles,
        near(live),
        code_parts,
        near(mixed),
        near(one),
        near(own),
        near(hot) if resident else hot[:16, :128],
        flops=2 * columns * pairs * strings * strings,
        in_specs=[vmem, code_spec, tiled((part, both, strings), 0)] + [vmem] * 3,
        out_shape=(shape_of((rows, columns), F32),)
        + tuple(shape_of((strings // 2 // pieces, columns), BF16) for _ in range(pieces)),
        out_specs=(vmem,) * (1 + pieces),
        scratch_shapes=[pltpu.VMEM((strings // 2, columns), F32)],
    )
    sides = list(sides) + [over_alpha(side, 1) for side in sides]
    return call(
        functools.partial(final_kernel, peers, lambda: (alpha() % 2, beta())),
        "final",
        1,
        near(alive),
        near(own),
        near(gathered),
        near(message),
        near(block),
        *[near(m) for m in arrived],
        *[near(side) for side in sides],
        in_specs=[vmem] * (4 + peers + 2 * pieces),
        out_shape=jax.ShapeDtypeStruct((rows, columns), BF16),
        out_specs=vmem,
        scratch_shapes=[pltpu.VMEM((strings, columns), BF16)],
    )


def solution(mesh):
    placed = (P("aa", "ba"), P(), P(), P(), P(), P())
    sizes = (mesh.shape["aa"], mesh.shape["ba"])
    return jax.shard_map(
        functools.partial(per_device, sizes), mesh=mesh, in_specs=placed, out_specs=P("aa", "ba"), check_vma=False
    )
```

```python
import functools

import jax
import jax.numpy as jnp
from jax import lax
from jax.experimental import pallas as pl
from jax.experimental.pallas import tpu as pltpu
from jax.sharding import PartitionSpec as P

BF16 = jnp.bfloat16
F32 = jnp.float32
I32 = jnp.int32
I16 = jnp.int16
RESIDENT = 8 * 2**20
VMEM_LIMIT = 48 * 2**20
NEAR_LIMIT = 16 * 2**20
SIDE_PIECES = 2


def iota(shape, dim):
    return lax.broadcasted_iota(I32, shape, dim)


def dot(x, y):
    return jnp.dot(x, y, preferred_element_type=F32)


def dot_nt(x, y):
    return lax.dot_general(x, y, (((1,), (1,)), ((), ())), preferred_element_type=F32)


def live_ids(counts_ref, first, shape, dim, cap):
    ids = iota(shape, dim)
    block = ids // cap
    count = jnp.zeros(shape, I32)
    for j in range(shape[dim] // cap):
        count = jnp.where(block == j, counts_ref[first // cap + j], count)
    return jnp.where(ids - block * cap < count, ids + first + 1, -1)


def sign_of(code):
    return jnp.where(code > 0, 1.0, -1.0).astype(F32)


def by_chip(groups):
    return (0, 2, 1, *range(3, groups)) if groups > 2 else tuple(range(groups))


def by_start(peers):
    return (*range(2, peers), 1)


def turned(at, column, columns):
    return ((at // columns) ^ column) * columns + at % columns


def tables_kernel(cap, place, counts_hbm, irrep_hbm, code_hbm, integrals_hbm, gains_hbm, amplitudes_hbm, *refs):
    code_ref, live_ref, lane_ref, mixer_ref, alive_ref, amplitudes_ref = refs[:6]
    counts_ref, irrep_ref, integrals_ref, gains_ref, plain_ref, sems = refs[6:]
    pairs, strings = code_ref.shape
    rows, columns = amplitudes_ref.shape
    first_a, column = place()
    first_b = column * columns
    copies = [
        pltpu.make_async_copy(source, target, sems.at[i])
        for i, (source, target) in enumerate(
            (
                (irrep_hbm, irrep_ref),
                (integrals_hbm, integrals_ref),
                (gains_hbm, gains_ref),
                (counts_hbm, counts_ref),
                (code_hbm, plain_ref),
                (amplitudes_hbm, amplitudes_ref),
            )
        )
    ]
    for copy in copies:
        copy.start()
    wide = pairs * 8
    spread_q = jnp.where(iota((wide, pairs), 0) // 8 == iota((wide, pairs), 1), 1.0, 0.0).astype(BF16)
    spread_p = jnp.where(iota((pairs, wide), 1) % pairs == iota((pairs, wide), 0), 1.0, 0.0).astype(BF16)
    for copy in copies:
        copy.wait()
    irrep_p = jnp.zeros((pairs, pairs), I32)
    irrep_q = jnp.zeros((pairs, pairs), I32)
    for p in range(pairs):
        irrep_p = jnp.where(iota((pairs, pairs), 0) == p, irrep_ref[p], irrep_p)
        irrep_q = jnp.where(iota((pairs, pairs), 1) == p, irrep_ref[p], irrep_q)
    weights = jnp.where(irrep_p == irrep_q, integrals_ref[...].astype(F32), 0.0).astype(BF16)
    left = jnp.concatenate(
        [dot_nt(spread_q, weights), jnp.broadcast_to(gains_ref[...].astype(F32), (8, pairs))], 0
    ).astype(BF16)
    mixer = dot(left, spread_p)
    same = iota(mixer.shape, 0) % 8 == iota(mixer.shape, 1) // pairs
    mixer_ref[...] = jnp.where(same, mixer, 0.0).astype(BF16)
    within = iota((cap, 128), 0)
    for block in range(strings // cap):
        at = block * cap
        live_ref[pl.ds(at, cap), :] = jnp.where(within < counts_ref[block], within + (at + 1), -1)
    for k in range(strings // columns):
        at = pl.multiple_of((column ^ k) * columns, columns)
        code_ref[:, k * columns : (k + 1) * columns] = plain_ref[:, pl.ds(at, columns)]
        lane_ref[:, k * columns : (k + 1) * columns] = live_ids(counts_ref, at, (8, columns), 1, cap)
    live_a = live_ids(counts_ref, first_a, (rows, columns), 0, cap)
    live_b = live_ids(counts_ref, first_b, (1, columns), 1, cap)
    alive_ref[...] = jnp.where((live_a > 0) & (live_b > 0), 1.0, 0.0)


def join_kernel(own_ref, sibling_ref, message_ref):
    rows = own_ref.shape[0]
    message_ref[:rows] = own_ref[...]
    message_ref[rows:] = sibling_ref[...]


def mix_kernel(columns_at, code_ref, lane_ref, mixer_ref, after_ref, mixed_ref, one_ref):
    pairs, strings = code_ref.shape
    wide = pairs * 8
    ids = jnp.broadcast_to(lane_ref[:1, :], (pairs, strings)).astype(I16)
    zero = jnp.zeros(ids.shape, BF16)
    mixer = mixer_ref[...]
    code = columns_at(code_ref)
    size = jnp.abs(code)
    sign = sign_of(code)

    def along(table, at, dtype):
        tile = jnp.broadcast_to(table[:, at : at + 1], (pairs, 128)).astype(dtype)
        return jnp.concatenate([tile] * (strings // 128), 1)

    for base in range(0, code.shape[1], 16):
        halves = []
        for low in (base, base + 8):
            hot = jnp.concatenate(
                [
                    jnp.where(along(size, a, I16) == ids, along(sign, a, BF16), zero)
                    for a in range(low, low + 8)
                ],
                0,
            )
            part = dot(mixer, hot)
            one_ref[pl.ds(low, 8), :] = part[wide:]
            halves.append(part[:wide].reshape(pairs, 8, strings))
        mixed_ref[:, pl.ds(base, 16), :] = jnp.concatenate(halves, 1).astype(BF16)


def hot_tile(code, ids):
    rows, strings = ids.shape
    size = jnp.broadcast_to(jnp.abs(code), (16, strings)).astype(I16)
    sign = jnp.broadcast_to(sign_of(code), (16, strings)).astype(BF16)
    size = jnp.concatenate([size] * (rows // 16), 0)
    sign = jnp.concatenate([sign] * (rows // 16), 0)
    return jnp.where(size == ids, sign, jnp.zeros(ids.shape, BF16))


def row_ids(live_ref, first, rows, strings):
    return jnp.concatenate([live_ref[pl.ds(first, rows), :]] * (strings // 128), 1).astype(I16)


def hot_kernel(steps, place, live_ref, code_ref, mixed_ref, one_ref, hot_ref, block_ref, total_ref):
    pairs, strings = code_ref.shape
    rows, columns = block_ref.shape
    step = 0 if steps == 1 else pl.program_id(0)
    column = place()
    first = pl.multiple_of(column * columns, columns)
    ids = row_ids(live_ref, first, columns, strings)
    if steps > 1:

        @pl.when(step == 0)
        def _():
            total_ref[...] = jnp.zeros_like(total_ref)

    total = jnp.zeros((columns, rows), F32) if steps == 1 else total_ref[...]
    for q in range(pairs):
        hot = hot_tile(code_ref[q : q + 1, :], ids)
        hot_ref[pl.ds(q * columns, columns), :] = hot
        total = total + dot_nt(hot, mixed_ref[q, :rows, :])
    if steps > 1:
        total_ref[...] = total
    block_ref[...] = (one_ref[:rows, :columns] + 0.5 * jnp.transpose(total)).astype(BF16)


def mixed_kernel(steps, groups, peers, place, mixed_ref, hot_ref, block_ref, *refs):
    arrived = [refs[by_chip(groups).index(k)] for k in range(groups)]
    own_ref, amplitudes_ref = refs[groups : groups + 2]
    sent = [refs[groups + 2 + by_start(peers).index(k)] for k in range(1, peers)]
    line, total_ref = refs[groups + 1 + peers :]
    pairs, strings = mixed_ref.shape[0], mixed_ref.shape[2]
    rows, columns = block_ref.shape
    step = 0 if steps == 1 else pl.program_id(0)
    group, core, column = place()

    @pl.when(step == 0)
    def _():
        if steps > 1:
            total_ref[...] = jnp.zeros_like(total_ref)
        for k in range(groups):
            first = (group ^ k) * 2
            at = pl.multiple_of(turned((first + core) * rows, column, columns), rows)
            amplitudes_ref[pl.ds(at, rows), :] = arrived[k][:rows]
            at = pl.multiple_of(turned((first + 1 - core) * rows, column, columns), rows)
            amplitudes_ref[pl.ds(at, rows), :] = arrived[k][rows:]

    if steps == 1:
        line = own_ref
    amplitudes = amplitudes_ref[...]
    for low in range(0, pairs, 4):
        part = dot(mixed_ref[low : low + 4, :rows, :].reshape(4 * rows, strings), amplitudes).astype(BF16)
        for q in range(4):
            line[:, pl.ds((low + q) * columns, columns)] = part[q * rows : (q + 1) * rows]
    if steps == 1:
        total = dot(line[...], hot_ref[:, columns:])
    else:
        total_ref[...] += dot(line[...], hot_ref[...])

    @pl.when(step == steps - 1)
    def _():
        if steps > 1:
            own_ref[...] = total_ref[:, :columns]
        for k in range(1, peers):
            if steps == 1:
                part = total[:, (k - 1) * columns : k * columns]
            else:
                part = total_ref[:, pl.ds(k * columns, columns)]
            sent[k - 1][:rows] = part.astype(BF16)
            sent[k - 1][rows : 2 * rows] = arrived[0][:rows]
            sent[k - 1][2 * rows :] = block_ref[...]


def same_spin_kernel(steps, place, live_ref, code_ref, mixed_ref, one_ref, part_ref, hot_ref, *refs):
    pairs, both, strings = mixed_ref.shape
    own_ref, side_refs, total_ref = refs[0], refs[1:-1], refs[-1]
    piece, columns = side_refs[0].shape
    half = piece * len(side_refs)
    step = 0 if steps == 1 else pl.program_id(0)
    core, column = place()
    at = pl.multiple_of(core * half, half)
    width = min(piece, columns)
    tile = piece
    if steps == 1:
        own_ref[...] = dot(part_ref[...], hot_ref[:, :columns])
    else:
        own_ref[...] = part_ref[...]
    if steps > 1:

        @pl.when(step == 0)
        def _():
            total_ref[...] = jnp.zeros_like(total_ref)

    for first in range(0, half, tile):
        ids = row_ids(live_ref, at + first, tile, strings)
        total = jnp.zeros((tile, columns), F32) if steps == 1 else total_ref[pl.ds(first, tile), :]
        for q in range(pairs):
            total = total + dot_nt(hot_tile(code_ref[q : q + 1, :], ids), mixed_ref[q, both - columns :, :])
        if steps > 1:
            total_ref[pl.ds(first, tile), :] = total
        blocks = [
            one_ref[both - columns :, pl.ds(pl.multiple_of(turned(at + low, column, columns), width), width)]
            for low in range(first, first + tile, width)
        ]
        one = jnp.transpose(jnp.concatenate(blocks, 1))
        side_refs[first // piece][...] = (one + 0.5 * total).astype(BF16)


def final_kernel(peers, place, alive_ref, own_ref, amplitudes_ref, message_ref, block_ref, *refs):
    out_ref, side_ref = refs[-2:]
    arrived, sides = [refs[by_start(peers).index(k)] for k in range(1, peers)], refs[peers - 1 : -2]
    rows, columns = own_ref.shape
    piece = sides[0].shape[0]
    pieces = len(sides) // 2
    core, column = place()
    for i in range(pieces):
        side_ref[pl.ds(pl.multiple_of((core * pieces + i) * piece, piece), piece), :] = sides[i][...]
        at = pl.multiple_of(((1 - core) * pieces + i) * piece, piece)
        side_ref[pl.ds(at, piece), :] = sides[pieces + i][...]
    total = own_ref[...]
    left, right = [], []
    for k in range(peers):
        at = pl.multiple_of((column ^ k) * columns, columns)
        if k == 0:
            left += [block_ref[...], message_ref[:rows]]
        else:
            left += [arrived[k - 1][2 * rows :], arrived[k - 1][rows : 2 * rows]]
            total = total + arrived[k - 1][:rows].astype(F32)
        right += [amplitudes_ref[k * columns : (k + 1) * columns, :], side_ref[pl.ds(at, columns), :]]
    total = total + dot(jnp.concatenate(left, 1), jnp.concatenate(right, 0))
    out_ref[...] = (total * alive_ref[...]).astype(BF16)


def per_device(sizes, amplitudes, code, counts, pair_irrep, integrals, one_body):
    rows, columns = amplitudes.shape
    pairs, strings = code.shape
    cap = strings // counts.shape[0]
    groups, peers = sizes[0] // 2, sizes[1]
    both = rows + columns
    resident = pairs * both * strings * 2 <= RESIDENT
    tile = both if resident else 128
    row_tiles = both // tile
    pair_tiles = 1 if resident else pairs // 4
    part = pairs // pair_tiles
    hbm = pl.BlockSpec(memory_space=pl.ANY)
    vmem = pl.BlockSpec(memory_space=pltpu.VMEM)

    def tiled(shape, dim):
        if resident:
            return vmem
        return pl.BlockSpec(shape, lambda i: tuple(i if d == dim else 0 for d in range(len(shape))))

    def shape_of(shape, dtype):
        return pltpu.VMEM(shape, dtype) if resident else jax.ShapeDtypeStruct(shape, dtype)

    def near(value):
        return pltpu.with_memory_space_constraint(value, pltpu.VMEM) if resident else value

    def far(value):
        return pltpu.with_memory_space_constraint(value, pltpu.HBM)

    def call(body, name, tiles, *args, flops=0, **keys):
        if tiles > 1:
            keys["grid"] = (tiles,)
        params = pltpu.CompilerParams(vmem_limit_bytes=NEAR_LIMIT if resident else VMEM_LIMIT)
        cost = pl.CostEstimate(flops=flops, bytes_accessed=0, transcendentals=0)
        return pl.pallas_call(body, name=name, compiler_params=params, cost_estimate=cost, **keys)(*args)

    def alpha():
        return lax.axis_index("aa")

    def beta():
        return lax.axis_index("ba")

    def over_alpha(value, mask):
        return lax.ppermute(value, "aa", [(i, i ^ mask) for i in range(sizes[0])])

    def over_beta(value, mask):
        return lax.ppermute(value, "ba", [(i, i ^ mask) for i in range(peers)])

    def columns_at(code_ref):
        if resident:
            at = turned(alpha() // 2 * 2 * rows, beta(), columns)
            chip = code_ref[:, pl.ds(pl.multiple_of(at, 2 * rows), 2 * rows)]
            own = jnp.where(alpha() % 2 == 0, chip[:, :rows], chip[:, rows:])
            return jnp.concatenate([own, code_ref[:, :columns]], 1)
        at = pl.program_id(0) * tile
        first = jnp.where(at < rows, alpha() * rows + at, beta() * columns + at - rows)
        return code_ref[:, pl.ds(pl.multiple_of(turned(first, beta(), columns), tile), tile)]

    sibling = over_alpha(amplitudes, 1)
    codes, live, lane, mixer, alive, own_c = call(
        functools.partial(tables_kernel, cap, lambda: (alpha() * rows, beta())),
        "tables",
        1,
        far(counts),
        far(pair_irrep),
        far(code),
        far(integrals),
        far(one_body.reshape(1, pairs)),
        far(amplitudes),
        in_specs=[hbm] * 6,
        out_shape=(
            shape_of((pairs, strings), I32),
            shape_of((strings, 128), I32),
            shape_of((8, strings), I32),
            shape_of((pairs * 8 + 8, pairs * 8), BF16),
            shape_of((rows, columns), F32),
            shape_of((rows, columns), BF16),
        ),
        out_specs=(vmem,) * 6,
        scratch_shapes=[
            pltpu.SMEM(counts.shape, I32),
            pltpu.SMEM(pair_irrep.shape, I32),
            pltpu.VMEM((pairs, pairs), BF16),
            pltpu.VMEM((1, pairs), BF16),
            pltpu.VMEM((pairs, strings), I32),
            pltpu.SemaphoreType.DMA((6,)),
        ],
    )
    message = call(
        join_kernel,
        "join",
        1,
        near(own_c),
        near(sibling),
        in_specs=[vmem] * 2,
        out_shape=shape_of((2 * rows, columns), BF16),
        out_specs=vmem,
    )
    messages = [message] + [over_alpha(message, 2 * k) for k in range(1, groups)]
    mixed, one = call(
        functools.partial(mix_kernel, columns_at),
        "mix",
        row_tiles,
        near(codes),
        near(lane),
        near(mixer),
        near(message),
        flops=2 * both * pairs * pairs * 8 * strings,
        in_specs=[vmem] * 4,
        out_shape=(shape_of((pairs, both, strings), BF16), shape_of((both, strings), F32)),
        out_specs=(tiled((pairs, tile, strings), 1), tiled((tile, strings), 0)),
    )
    code_parts = near(codes) if resident else codes.reshape(pair_tiles, part, strings)
    code_spec = vmem if resident else pl.BlockSpec((None, part, strings), lambda i: (i, 0, 0))
    hot, block = call(
        functools.partial(hot_kernel, pair_tiles, beta),
        "hot",
        pair_tiles,
        near(live),
        code_parts,
        near(mixed),
        near(one),
        flops=2 * pairs * rows * columns * strings,
        in_specs=[vmem, code_spec, tiled((part, both, strings), 0), vmem],
        out_shape=(shape_of((pairs * columns, strings), BF16), shape_of((rows, columns), BF16)),
        out_specs=(tiled((part * columns, strings), 0), vmem),
        scratch_shapes=[pltpu.VMEM((columns, rows), F32)],
    )
    outs = call(
        functools.partial(mixed_kernel, pair_tiles, groups, peers, lambda: (alpha() // 2, alpha() % 2, beta())),
        "mixed",
        pair_tiles,
        near(mixed),
        near(hot),
        near(block),
        *[near(messages[k]) for k in by_chip(groups)],
        in_specs=[tiled((part, both, strings), 0), tiled((part * columns, strings), 0)] + [vmem] * (groups + 1),
        out_shape=(
            shape_of((rows, pairs * columns), BF16) if resident else shape_of((rows, columns), F32),
            shape_of((strings, columns), BF16),
        )
        + tuple(shape_of((3 * rows, columns), BF16) for _ in range(peers - 1)),
        out_specs=(vmem,) * (peers + 1),
        scratch_shapes=[pltpu.VMEM((rows, part * columns), BF16), pltpu.VMEM((rows, strings), F32)],
    )
    own, gathered = outs[:2]
    arrived = [over_beta(m, k) for k, m in zip(by_start(peers), outs[2:])]
    pieces = SIDE_PIECES
    own, *sides = call(
        functools.partial(same_spin_kernel, pair_tiles, lambda: (alpha() % 2, beta())),
        "same_spin",
        pair_tiles,
        near(live),
        code_parts,
        near(mixed),
        near(one),
        near(own),
        near(hot) if resident else hot[:16, :128],
        flops=2 * columns * pairs * strings * strings,
        in_specs=[vmem, code_spec, tiled((part, both, strings), 0)] + [vmem] * 3,
        out_shape=(shape_of((rows, columns), F32),)
        + tuple(shape_of((strings // 2 // pieces, columns), BF16) for _ in range(pieces)),
        out_specs=(vmem,) * (1 + pieces),
        scratch_shapes=[pltpu.VMEM((strings // 2, columns), F32)],
    )
    sides = list(sides) + [over_alpha(side, 1) for side in sides]
    return call(
        functools.partial(final_kernel, peers, lambda: (alpha() % 2, beta())),
        "final",
        1,
        near(alive),
        near(own),
        near(gathered),
        near(message),
        near(block),
        *[near(m) for m in arrived],
        *[near(side) for side in sides],
        in_specs=[vmem] * (4 + peers + 2 * pieces),
        out_shape=jax.ShapeDtypeStruct((rows, columns), BF16),
        out_specs=vmem,
        scratch_shapes=[pltpu.VMEM((strings, columns), BF16)],
    )


def solution(mesh):
    placed = (P("aa", "ba"), P(), P(), P(), P(), P())
    sizes = (mesh.shape["aa"], mesh.shape["ba"])
    return jax.shard_map(
        functools.partial(per_device, sizes), mesh=mesh, in_specs=placed, out_specs=P("aa", "ba"), check_vma=False
    )
```
